32 devices in a mesh: groups: 2 (over x), inst: 2 (over core), tp: 8 (over z, y).
Axes of the slice: x: 2, y: 2, z: 4, core: 2. Of those that a mesh axis runs over, the one named last changes fastest.
Arguments:
- hidden_input: bfloat16 [4, 16, 8192], P(None, ('groups', 'inst')), parts along dimension 1, may hold values from -6 to 6
- input_norm_gain: bfloat16 [8192], replicated, may hold values from 0.25 to 1.75
- query_weight: bfloat16 [8192, 8192], P(None, 'tp'), may hold values from -0.0625 to 0.0625
- key_weight: bfloat16 [8192, 1024], P(None, 'tp'), may hold values from -0.0625 to 0.0625
- value_weight: bfloat16 [8192, 1024], P(None, 'tp'), may hold values from -0.0625 to 0.0625
- output_weight: bfloat16 [8192, 8192], P('tp'), may hold values from -0.09375 to 0.09375
- key_value_cache: bfloat16 [16, 512, 2048], P(('groups', 'inst'), 'tp'), parts along dimension 0, may hold values from -320 to 320
- lengths: int32 [16], P('groups'), parts along dimension 0, may hold values from 64 to 512, as said below
- leaving: int32 [4, 2], P('groups'), parts along dimension 0, may hold values from 0 to 3, as said below
- request_adapter_index: int32 [16], P('groups'), parts along dimension 0, may hold values from 0 to 31
- adapter_page_table: int32 [32], replicated, may hold values from 0 to 31, each once
- adapter_down_pages: bfloat16 [32, 8192, 64], P('inst', 'tp'), may hold values from -0.0625 to 0.0625
- adapter_up_pages: bfloat16 [32, 64, 8192], P('inst', None, 'tp'), may hold values from -0.75 to 0.75
Outputs:
- layer_out: bfloat16 [4, 16, 8192], P(None, ('groups', 'inst'), 'tp'), parts along dimension 1
The draws below stay inside these ranges and needn't reach their ends.
There are 2 independent parts, one for each index of `groups`. The reference program is written for one: setup_inputs(seed, part) draws one part's arguments, and reference() takes and returns one part's arrays. A program takes and returns all parts, laid end to end along the dimension named above; an argument that names none is the same for every part. Nothing has to cross between parts.
Inputs may be any that keep to these rules, and one draw needn't show every extreme that they name: `lengths`: some request has exactly 512 cached positions. `leaving`: each row lists 2 different slots.
All inputs are finite; a program needn't handle non-finite values.
Results may differ from the reference program's by a relative error of at most 0.039.
Values may be sent and summed in bfloat16 or wider, within the bound.
A program may use at most 128 MiB of HBM per device.

```python
import math
import jax
import jax.numpy as jnp
import numpy as np
from jax import lax

MODEL_WIDTH = 8192
QUERY_HEADS = 64
KVH = 8
HEAD_SIZE = 128
ADAPTER_RANK = 64
STEPS = 4
MIG = 2
R_INST = 4
REQS = 8
LEN = 512
ADAPTER_COUNT = 32


def draw_key_value_cache(key, part):
    key = jax.random.fold_in(key, 11)
    base_key = jax.random.fold_in(key, 0)
    values = jnp.clip(jax.random.normal(base_key, (REQS, LEN, 2 * KVH * HEAD_SIZE), jnp.float32), -4.0, 4.0)
    return values.astype(jnp.bfloat16)


def draw_lengths(key, part):
    key = jax.random.fold_in(key, 12)
    first_key, second_key = jax.random.split(key)
    values = jax.random.randint(first_key, (REQS,), LEN // 8, LEN + 1)
    longest = jax.random.randint(second_key, (), 0, REQS)
    return jnp.where(jnp.arange(REQS) == longest, LEN, values).astype(jnp.int32)


def draw_leaving(key, part):
    key = jax.random.fold_in(key, 13)
    first_key, second_key = jax.random.split(key)
    first_row = jax.random.permutation(first_key, R_INST)[:MIG].astype(jnp.int32)
    second_row = jax.random.permutation(second_key, R_INST)[:MIG].astype(jnp.int32)
    return jnp.stack([first_row, second_row]).astype(jnp.int32)


def with_ends(drawn, own_key, least, high):
    index_at = [jax.random.randint(jax.random.fold_in(own_key, axis), (), 0, length) for axis, length in enumerate(drawn.shape)]
    main_axis = drawn.shape.index(max(drawn.shape))
    next_to = index_at[:main_axis] + [(index_at[main_axis] + 1) % drawn.shape[main_axis]] + index_at[main_axis + 1:]
    return drawn.at[tuple(index_at)].set(least).at[tuple(next_to)].set(high)


def spiked(drawn, rng, source, target, shards_of, factor):
    owner, partner = [(jnp.arange(drawn.shape[axis_at]) // (drawn.shape[axis_at] // shards_of)).reshape([-1 if axis == axis_at else 1 for axis in range(drawn.ndim)]) for axis_at in (source, target)]
    chosen = jax.random.permutation(rng, shards_of)[partner]
    strong = (owner == chosen) | (owner == (partner + shards_of // 2) % shards_of)
    return jnp.where(strong, factor * drawn, drawn)


def shard_levels(own_key, dims, pieces, low, largest):
    loudness = 1.0
    for dim, parts in pieces:
        heights = jax.random.uniform(jax.random.fold_in(jax.random.fold_in(own_key, 6), dim), (parts,), jnp.float32, low / len(pieces), largest / len(pieces))
        loudness = loudness * jnp.repeat(jnp.exp(heights), dims[dim] // parts).reshape((-1,) + (1,) * (len(dims) - 1 - dim))
    return loudness


def rank_bounds(amount, slope):
    loads = [(1 << 20) // math.isqrt(grade ** slope) + 1 for grade in range(1, amount + 1)]
    scale = 1 + sum(loads) // (1 << 30)
    return np.cumsum(np.array([max(1, weight // scale) for weight in loads]))


def ranked(own_key, extent, number_of, lean):
    grid = rank_bounds(number_of, lean)
    pick = jax.random.randint(jax.random.fold_in(own_key, 1), extent, 0, int(grid[number_of - 1]))
    grade = jnp.searchsorted(jnp.asarray(grid, jnp.int32), pick, side="right")
    return jax.random.permutation(jax.random.fold_in(own_key, 2), number_of)[grade].astype(jnp.int32)


def bell_draw(key, shape, deviation, most, shards=(), kind=jnp.bfloat16):
    values = jax.random.normal(key, shape, jnp.float32) * deviation
    if len(shards) > 0:
        values = shard_levels(key, shape, shards, -0.22, 0.18) * values
    return jnp.clip(values, min=-most, max=most).astype(kind)


def bell_draw_with(key, dims, scale, most, cuts, heavy, kind=jnp.bfloat16):
    array = scale * jax.random.normal(key, dims, jnp.float32)
    if cuts:
        array = array * shard_levels(key, dims, cuts, -0.22, 0.18)
    return jnp.clip(spiked(array, jax.random.fold_in(key, 3), *heavy), -most, most).astype(kind)


def setup_inputs(seed: int = 0, part: int = 0) -> dict:
    splits = jax.random.split(jax.random.key(seed), 14)
    part_splits = jax.random.split(jax.random.fold_in(splits[13], part), 14)
    hidden_input = bell_draw(part_splits[0], (STEPS, REQS, MODEL_WIDTH), 1.0, 6.0, ((1, 2),))
    input_norm_gain = jnp.clip(1.0 + 0.15 * jax.random.normal(splits[1], (MODEL_WIDTH,), jnp.float32), 0.25, 1.75).astype(jnp.bfloat16)
    query_weight = bell_draw(splits[2], (MODEL_WIDTH, QUERY_HEADS * HEAD_SIZE), MODEL_WIDTH ** -0.5, 0.0625, ((1, 8),))
    key_weight = bell_draw(splits[3], (MODEL_WIDTH, KVH * HEAD_SIZE), MODEL_WIDTH ** -0.5, 0.0625, ((1, 8),))
    value_weight = bell_draw(splits[4], (MODEL_WIDTH, KVH * HEAD_SIZE), MODEL_WIDTH ** -0.5, 0.0625, ((1, 8),))
    output_weight = bell_draw_with(splits[5], (QUERY_HEADS * HEAD_SIZE, MODEL_WIDTH), (QUERY_HEADS * HEAD_SIZE) ** -0.5, 0.09375, ((0, 8),), (0, 1, 8, 2.0))
    key_value_cache = draw_key_value_cache(jax.random.fold_in(jax.random.fold_in(splits[13], part), 71), part)
    lengths = draw_lengths(jax.random.fold_in(jax.random.fold_in(splits[13], part), 71), part)
    leaving = draw_leaving(jax.random.fold_in(jax.random.fold_in(splits[13], part), 71), part)
    request_adapter_index = with_ends(ranked(part_splits[9], (REQS,), ADAPTER_COUNT, 2), jax.random.fold_in(part_splits[9], 3), 0, ADAPTER_COUNT - 1).astype(jnp.int32)
    adapter_page_table = jax.random.permutation(splits[10], ADAPTER_COUNT).astype(jnp.int32)
    adapter_down_pages = bell_draw(splits[11], (ADAPTER_COUNT, QUERY_HEADS * HEAD_SIZE, ADAPTER_RANK), (QUERY_HEADS * HEAD_SIZE) ** -0.5, 0.0625, ((0, 2), (1, 8)))
    adapter_up_pages = bell_draw(splits[12], (ADAPTER_COUNT, ADAPTER_RANK, MODEL_WIDTH), ADAPTER_RANK ** -0.5, 0.75, ((0, 2), (2, 8)))
    return {"hidden_input": hidden_input, "input_norm_gain": input_norm_gain, "query_weight": query_weight, "key_weight": key_weight, "value_weight": value_weight, "output_weight": output_weight, "key_value_cache": key_value_cache, "lengths": lengths, "leaving": leaving, "request_adapter_index": request_adapter_index, "adapter_page_table": adapter_page_table, "adapter_down_pages": adapter_down_pages, "adapter_up_pages": adapter_up_pages}


THETA = 500000.0
ADAPTER_SCALE = 0.5
NEGATIVE = -1e+30

def normalize(hidden, input_norm_gain):
    values = hidden.astype(jnp.float32)
    factor = lax.rsqrt(lax.optimization_barrier(jnp.mean(values * values, axis=-1, keepdims=True)) + 1e-05)
    return (values * factor * input_norm_gain.astype(jnp.float32)).astype(jnp.bfloat16)

def rotate(tensor, position):
    middle = tensor.shape[-1] // 2
    freqs = jnp.exp(jnp.arange(middle, dtype=jnp.float32) * (-2.0 * math.log(THETA) / tensor.shape[-1]))
    angles = position[..., None] * freqs
    cosine = jnp.cos(angles)
    sine_part = jnp.sin(angles)
    first = tensor[..., :middle]
    second = tensor[..., middle:]
    return jnp.concatenate([first * cosine - second * sine_part, second * cosine + first * sine_part], axis=-1)

def reference(hidden_input, input_norm_gain, query_weight, key_weight, value_weight, output_weight, key_value_cache, lengths, leaving, request_adapter_index, adapter_page_table, adapter_down_pages, adapter_up_pages):
    decode_steps, requests, width = hidden_input.shape
    group = QUERY_HEADS // KVH
    kv_width = KVH * HEAD_SIZE
    normed = normalize(hidden_input, input_norm_gain).reshape(decode_steps * requests, width)
    query = jnp.dot(normed, query_weight, preferred_element_type=jnp.float32).astype(jnp.bfloat16)
    key_new = jnp.dot(normed, key_weight, preferred_element_type=jnp.float32).astype(jnp.bfloat16)
    value_new = jnp.dot(normed, value_weight, preferred_element_type=jnp.float32).astype(jnp.bfloat16)
    new_pos = (lengths[None, :] + jnp.arange(decode_steps, dtype=jnp.int32)[:, None]).astype(jnp.float32)[:, :, None]
    query_rot = rotate(query.reshape(decode_steps, requests, QUERY_HEADS, HEAD_SIZE).astype(jnp.float32), new_pos).astype(jnp.bfloat16)
    key_rot = rotate(key_new.reshape(decode_steps, requests, KVH, HEAD_SIZE).astype(jnp.float32), new_pos).astype(jnp.bfloat16)
    value_new = value_new.reshape(decode_steps, requests, KVH, HEAD_SIZE)
    source = jnp.arange(requests, dtype=jnp.int32)
    source = source.at[leaving[0]].set(R_INST + leaving[1])
    source = source.at[R_INST + leaving[1]].set(leaving[0])
    pages = adapter_page_table[request_adapter_index]
    inverse = 1.0 / math.sqrt(HEAD_SIZE)
    causal = jnp.arange(decode_steps)[None, :] <= jnp.arange(decode_steps)[:, None]
    causal_b = causal[:, None, None, :]

    def one_request(slot):
        cache_rows = key_value_cache[source[slot]]
        keys = cache_rows[:, :kv_width].reshape(LEN, KVH, HEAD_SIZE).astype(jnp.float32)
        values = cache_rows[:, kv_width:].reshape(LEN, KVH, HEAD_SIZE).astype(jnp.float32)
        query_here = query_rot[:, slot].reshape(decode_steps, KVH, group, HEAD_SIZE).astype(jnp.float32)
        valid = jnp.arange(LEN, dtype=jnp.int32) < lengths[slot]
        valid_b = valid[None, None, None, :]
        cache_scores = jnp.einsum('skgd,pkd->skgp', query_here, keys) * inverse
        cache_scores = jnp.where(valid_b, cache_scores, NEGATIVE)
        new_scores = jnp.einsum('skgd,tkd->skgt', query_here, key_rot[:, slot].astype(jnp.float32)) * inverse
        new_scores = jnp.where(causal_b, new_scores, NEGATIVE)
        top = jnp.maximum(cache_scores.max(-1), new_scores.max(-1))
        cache_weights = jnp.exp(cache_scores - top[..., None]) * valid_b.astype(jnp.float32)
        new_weights = jnp.exp(new_scores - top[..., None]) * causal_b.astype(jnp.float32)
        total = cache_weights.sum(-1) + new_weights.sum(-1)
        cache_round = lax.optimization_barrier(cache_weights.astype(jnp.bfloat16)).astype(jnp.float32)
        new_round = lax.optimization_barrier(new_weights.astype(jnp.bfloat16)).astype(jnp.float32)
        mixed = jnp.einsum('skgp,pkd->skgd', cache_round, values)
        mixed = mixed + jnp.einsum('skgt,tkd->skgd', new_round, value_new[:, slot].astype(jnp.float32))
        attention_output = (mixed / total[..., None]).astype(jnp.bfloat16).reshape(decode_steps, QUERY_HEADS * HEAD_SIZE)
        store_page = pages[slot]
        shrunk_output = jnp.dot(attention_output, adapter_down_pages[store_page], preferred_element_type=jnp.float32).astype(jnp.bfloat16)
        adapter_delta = jnp.dot(shrunk_output, adapter_up_pages[store_page], preferred_element_type=jnp.float32)
        base_output = jnp.dot(attention_output, output_weight, preferred_element_type=jnp.float32)
        return (base_output + ADAPTER_SCALE * adapter_delta).astype(jnp.bfloat16)
    result = lax.map(one_request, jnp.arange(requests, dtype=jnp.int32))
    return jnp.transpose(result, (1, 0, 2))
```

```python
import functools
import math

import jax
import jax.numpy as jnp
from jax import lax
from jax.experimental import pallas as pl
from jax.experimental.pallas import tpu as pltpu
from jax.sharding import PartitionSpec as P

QUERY_HEADS = 64
KVH = 8
HEAD_SIZE = 128
MESH = pl.DeviceIdType.MESH


THETA = 500000.0
ADAPTER_SCALE = 0.5
NEGATIVE = -1e30


def partner(block, axis, bit):
    count = lax.axis_size(axis)
    route = []
    for low in range(count):
        high = low | 1 << bit
        if high != low and high < count:
            route += [(low, high), (high, low)]
    return lax.ppermute(block, axis, route)


def combined_all(value, axis, combine):
    everything = jax.tree.map(
        lambda part, kind: lax.all_gather(part.astype(kind), axis),
        value,
        (jnp.bfloat16, jnp.bfloat16, jnp.bfloat16),
    )

    def take(k):
        return jax.tree.map(lambda part, own: part[k].astype(own.dtype), everything, value)

    return lax.fori_loop(
        1, lax.axis_size(axis), lambda k, so_far: combine(so_far, take(k)), take(0)
    )


def normalize(hidden, input_norm_gain):
    values = hidden.astype(jnp.float32)
    factor = lax.rsqrt(jnp.mean(values * values, axis=-1, keepdims=True) + 1e-05)
    return (values * factor * input_norm_gain.astype(jnp.float32)).astype(jnp.bfloat16)


def rotate(tensor, position):
    middle = tensor.shape[-1] // 2
    freqs = jnp.exp(
        jnp.arange(middle, dtype=jnp.float32) * (-2.0 * math.log(THETA) / tensor.shape[-1])
    )
    angles = position[..., None] * freqs
    cosine = jnp.cos(angles)
    sine_part = jnp.sin(angles)
    first = tensor[..., :middle]
    second = tensor[..., middle:]
    return jnp.concatenate(
        [first * cosine - second * sine_part, second * cosine + first * sine_part], axis=-1
    )


def combine(earlier, later):
    top_first, total_first, mixed_first = earlier
    top_second, total_second, mixed_second = later
    top = jnp.maximum(top_first, top_second)
    scale_first = jnp.exp(top_first - top)
    scale_second = jnp.exp(top_second - top)
    total = total_first * scale_first + total_second * scale_second
    mixed = mixed_first * scale_first[..., None] + mixed_second * scale_second[..., None]
    return (top, total, mixed)


def shards(
    hidden_input,
    input_norm_gain,
    query_weight,
    key_weight,
    value_weight,
    output_weight,
    key_value_cache,
    lengths,
    leaving,
    request_adapter_index,
    adapter_page_table,
    adapter_down_pages,
    adapter_up_pages,
):
    decode_steps, request_rows, width = hidden_input.shape
    device = lax.axis_index("tp")
    instance = lax.axis_index("inst")
    head_cols = query_weight.shape[1]
    local_heads = head_cols // HEAD_SIZE
    positions = key_value_cache.shape[1]
    kv_width = KVH * HEAD_SIZE
    group = QUERY_HEADS // KVH
    normed = normalize(hidden_input, input_norm_gain).reshape(decode_steps * request_rows, width)
    query_part = jnp.dot(normed, query_weight, preferred_element_type=jnp.float32).astype(
        jnp.bfloat16
    )
    key_part = jnp.dot(normed, key_weight, preferred_element_type=jnp.float32).astype(jnp.bfloat16)
    value_part = jnp.dot(normed, value_weight, preferred_element_type=jnp.float32).astype(
        jnp.bfloat16
    )
    query_all, key_all, value_all = (
        lax.all_gather(query_part, "tp", axis=1, tiled=True),
        lax.all_gather(key_part, "tp", axis=1, tiled=True),
        lax.all_gather(value_part, "tp", axis=1, tiled=True),
    )
    lengths_here = lax.dynamic_slice_in_dim(lengths, instance * request_rows, request_rows)
    new_pos = (lengths_here[None, :] + jnp.arange(decode_steps, dtype=jnp.int32)[:, None]).astype(
        jnp.float32
    )[:, :, None]
    query_rot = rotate(
        query_all.reshape(decode_steps, request_rows, QUERY_HEADS, HEAD_SIZE).astype(jnp.float32),
        new_pos,
    ).astype(jnp.bfloat16)
    query_rot = query_rot.reshape(decode_steps, request_rows, KVH, group, HEAD_SIZE)
    key_rot = rotate(
        key_all.reshape(decode_steps, request_rows, KVH, HEAD_SIZE).astype(jnp.float32), new_pos
    ).astype(jnp.bfloat16)
    value_new = value_all.reshape(decode_steps, request_rows, KVH, HEAD_SIZE)
    outgoing_slots = lax.dynamic_index_in_dim(leaving, instance, 0, keepdims=False)
    arriving = partner(key_value_cache[outgoing_slots], "inst", 0)
    cache_now = key_value_cache.at[outgoing_slots].set(arriving)
    pages = adapter_page_table[request_adapter_index]
    adapter_store_size = adapter_down_pages.shape[0]
    own_pages = lax.dynamic_slice_in_dim(pages, instance * request_rows, request_rows)
    partner_pages = lax.dynamic_slice_in_dim(pages, (1 - instance) * request_rows, request_rows)

    def select_pages(wanted):
        local_page_index = jnp.clip(
            wanted - instance * adapter_store_size, 0, adapter_store_size - 1
        )
        down_matrix_flat = adapter_down_pages[local_page_index].reshape(request_rows, -1)
        up_matrix_flat = adapter_up_pages[local_page_index].reshape(request_rows, -1)
        return (
            jnp.concatenate([down_matrix_flat, up_matrix_flat], axis=1),
            wanted // adapter_store_size == instance,
        )

    outgoing_pages, held_there = select_pages(partner_pages)
    outgoing_pages = jnp.where(held_there[:, None], outgoing_pages, jnp.zeros_like(outgoing_pages))
    arriving_pages = partner(outgoing_pages, "inst", 0)
    local_pages, held_here = select_pages(own_pages)
    fetched_pages = jnp.where(held_here[:, None], local_pages, arriving_pages)
    down_matrix_size = adapter_down_pages.shape[1] * adapter_down_pages.shape[2]
    down_matrix_rows = fetched_pages[:, :down_matrix_size].reshape(
        request_rows, adapter_down_pages.shape[1], adapter_down_pages.shape[2]
    )
    up_matrix_rows = fetched_pages[:, down_matrix_size:].reshape(
        request_rows, adapter_up_pages.shape[1], adapter_up_pages.shape[2]
    )
    keys = cache_now[:, :, :kv_width].reshape(request_rows, positions, KVH, HEAD_SIZE)
    values = cache_now[:, :, kv_width:].reshape(request_rows, positions, KVH, HEAD_SIZE)
    place = device * positions + jnp.arange(positions, dtype=jnp.int32)
    valid = place[None, :] < lengths_here[:, None]
    valid_b = valid[None, :, None, None, :]
    inverse = 1.0 / math.sqrt(HEAD_SIZE)
    cache_scores = (
        jnp.einsum("srkgd,rpkd->srkgp", query_rot, keys, preferred_element_type=jnp.float32)
        * inverse
    )
    cache_scores = jnp.where(valid_b, cache_scores, NEGATIVE)
    new_scores = (
        jnp.einsum("srkgd,trkd->srkgt", query_rot, key_rot, preferred_element_type=jnp.float32)
        * inverse
    )
    causal = (jnp.arange(decode_steps)[None, :] <= jnp.arange(decode_steps)[:, None]) & (
        device == 0
    )
    causal_b = causal[:, None, None, None, :]
    new_scores = jnp.where(causal_b, new_scores, NEGATIVE)
    top = jnp.maximum(cache_scores.max(-1), new_scores.max(-1))
    cache_weights = jnp.exp(cache_scores - top[..., None]) * valid_b.astype(jnp.float32)
    new_weights = jnp.exp(new_scores - top[..., None]) * causal_b.astype(jnp.float32)
    total = cache_weights.sum(-1) + new_weights.sum(-1)
    mixed = jnp.einsum(
        "srkgp,rpkd->srkgd",
        cache_weights.astype(jnp.bfloat16),
        values,
        preferred_element_type=jnp.float32,
    )
    mixed = mixed + jnp.einsum(
        "srkgt,trkd->srkgd",
        new_weights.astype(jnp.bfloat16),
        value_new,
        preferred_element_type=jnp.float32,
    )
    top = top.reshape(decode_steps, request_rows, QUERY_HEADS)
    total = total.reshape(decode_steps, request_rows, QUERY_HEADS)
    mixed = mixed.reshape(decode_steps, request_rows, QUERY_HEADS, HEAD_SIZE)
    top_all, total_all, mixed_all = combined_all((top, total, mixed), "tp", combine)
    first_head = device * local_heads
    total_own = lax.dynamic_slice_in_dim(total_all, first_head, local_heads, 2)
    mixed_own = lax.dynamic_slice_in_dim(mixed_all, first_head, local_heads, 2)
    attention_output = mixed_own / total_own[..., None]
    attention_output = attention_output.astype(jnp.bfloat16).reshape(
        decode_steps * request_rows, head_cols
    )
    base_part = jnp.dot(attention_output, output_weight, preferred_element_type=jnp.float32)
    shrink_part = jnp.einsum(
        "src,rck->srk",
        attention_output.reshape(decode_steps, request_rows, head_cols),
        down_matrix_rows,
        preferred_element_type=jnp.float32,
    )
    shrunk_output = lax.psum(shrink_part, "tp")
    base_output = lax.psum_scatter(
        base_part.astype(jnp.bfloat16), "tp", scatter_dimension=1, tiled=True
    ).astype(jnp.float32)
    shrunk_output = shrunk_output.astype(jnp.bfloat16)
    adapter_delta = jnp.einsum(
        "srk,rkd->srd", shrunk_output, up_matrix_rows, preferred_element_type=jnp.float32
    )
    return (
        base_output.reshape(decode_steps, request_rows, -1) + ADAPTER_SCALE * adapter_delta
    ).astype(jnp.bfloat16)


def fused_kernel(
    dims,
    hidden_ref,
    gain_ref,
    wq_hbm,
    wk_hbm,
    wv_hbm,
    wo_hbm,
    cache_hbm,
    lengths_ref,
    leaving_ref,
    adapter_ref,
    table_ref,
    down_hbm,
    up_hbm,
    out_ref,
    wq,
    wk,
    wv,
    wo,
    cache,
    moved_out,
    moved_in,
    keys,
    values,
    down,
    up,
    down_out,
    up_out,
    down_in,
    up_in,
    hidden,
    normed,
    query_all,
    part_out,
    part_in,
    stat,
    stat_out,
    stat_in,
    shrink_part,
    shrink_in,
    base_out,
    base_in,
    wq_sem,
    wkv_sem,
    wo_sem,
    store_sem,
    pair_send,
    pair_recv,
    query_send,
    query_recv,
    part_send,
    part_recv,
    stat_send,
    stat_recv,
    shrink_send,
    shrink_recv,
    base_send,
    base_recv,
):
    n, steps, reqs, width, head_cols, positions, store, rank, out_cols, chunks, pieces = dims
    rows = steps * reqs
    head_count = head_cols // HEAD_SIZE
    chunk_heads = head_count // chunks
    chunk_cols = chunk_heads * HEAD_SIZE
    piece = width // pieces
    kv_width = n * HEAD_SIZE
    me = lax.axis_index("tp")
    inst = lax.axis_index("inst")
    other = 1 - inst
    f32, bf16 = jnp.float32, jnp.bfloat16
    inverse = 1.0 / math.sqrt(HEAD_SIZE)

    def each_peer(body):
        def step(o, carry):
            body(lax.rem(me + 1 + o, n))
            return carry

        lax.fori_loop(0, n - 1, step, 0)

    cache_copy = pltpu.make_async_copy(cache_hbm, cache, store_sem.at[0])
    cache_copy.start()
    wq_copies = {}
    for c in range(chunks):
        for k in range(pieces):
            at = (pl.ds(k * piece, piece), pl.ds(c * chunk_cols, chunk_cols))
            wq_copies[c, k] = pltpu.make_async_copy(
                wq_hbm.at[at], wq.at[at], wq_sem.at[c, k]
            )
            wq_copies[c, k].start()
    wk_copy = pltpu.make_async_copy(wk_hbm, wk, wkv_sem.at[0])
    wv_copy = pltpu.make_async_copy(wv_hbm, wv, wkv_sem.at[1])
    down_copy = pltpu.make_async_copy(down_hbm, down, store_sem.at[1])
    up_copy = pltpu.make_async_copy(up_hbm, up, store_sem.at[2])
    wk_copy.start()
    wv_copy.start()
    down_copy.start()
    up_copy.start()

    def wo_copy(p):
        cols = pl.ds(pl.multiple_of(p * out_cols, out_cols), out_cols)
        return pltpu.make_async_copy(wo_hbm.at[:, cols], wo.at[p], wo_sem.at[p])

    def start_wo(o, carry):
        wo_copy(lax.rem(me + 1 + o, n)).start()
        return carry

    lax.fori_loop(0, n, start_wo, 0)

    barrier = pltpu.get_barrier_semaphore()
    each_peer(lambda p: pl.semaphore_signal(barrier, inc=1, device_id={"tp": p}, device_id_type=MESH))
    pl.semaphore_signal(barrier, inc=1, device_id={"inst": other}, device_id_type=MESH)

    for s in range(steps):
        hidden[pl.ds(s * reqs, reqs), :] = hidden_ref[s].astype(f32)
    block = hidden[...]
    factor = lax.rsqrt(jnp.mean(block * block, axis=-1, keepdims=True) + 1e-05)
    normed[...] = (block * factor * gain_ref[...].astype(f32)).astype(bf16)

    own_lengths = [lengths_ref[inst * reqs + r] for r in range(reqs)]

    def by_request(index, numbers):
        chosen = jnp.full(index.shape, numbers[0], jnp.int32)
        for r in range(1, reqs):
            chosen = jnp.where(index == r, numbers[r], chosen)
        return chosen

    row = lax.broadcasted_iota(jnp.int32, (rows, HEAD_SIZE), 0)
    lane = lax.broadcasted_iota(jnp.int32, (rows, HEAD_SIZE), 1)
    half = HEAD_SIZE // 2
    place = (by_request(row & (reqs - 1), own_lengths) + row // reqs).astype(f32)
    freqs = jnp.exp((lane & (half - 1)).astype(f32) * (-2.0 * math.log(THETA) / HEAD_SIZE))
    angle = place * freqs
    cosine = jnp.cos(angle)
    sine = jnp.where(lane < half, -1.0, 1.0) * jnp.sin(angle)

    def rotated(tensor):
        return (tensor * cosine + pltpu.roll(tensor, half, 1) * sine).astype(bf16)

    cache_copy.wait()
    for j in range(2):
        moved_out[j] = cache[leaving_ref[inst, j]]
    pl.semaphore_wait(barrier, n)

    def pair(src, dst, k):
        return pltpu.make_async_remote_copy(
            src_ref=src,
            dst_ref=dst,
            send_sem=pair_send.at[k],
            recv_sem=pair_recv.at[k],
            device_id={"inst": other},
            device_id_type=MESH,
        )

    moving = pair(moved_out, moved_in, 0)
    moving.start()

    def query_copy(c, owner, p):
        return pltpu.make_async_remote_copy(
            src_ref=query_all.at[c, owner],
            dst_ref=query_all.at[c, owner],
            send_sem=query_send.at[c, p],
            recv_sem=query_recv.at[c, owner],
            device_id={"tp": p},
            device_id_type=MESH,
        )

    for c in range(chunks):
        total = jnp.zeros((rows, chunk_cols), f32)
        for k in range(pieces):
            wq_copies[c, k].wait()
            total += jnp.dot(
                normed[:, k * piece : (k + 1) * piece],
                wq[k * piece : (k + 1) * piece, c * chunk_cols : (c + 1) * chunk_cols],
                preferred_element_type=f32,
            )
        total = total.astype(bf16).astype(f32)
        for h in range(chunk_heads):
            query_all[c, me, h * rows : (h + 1) * rows, :] = rotated(
                total[:, h * HEAD_SIZE : (h + 1) * HEAD_SIZE]
            )
        each_peer(lambda p: query_copy(c, me, p).start())

    moving.wait_recv()
    first, second = leaving_ref[inst, 0], leaving_ref[inst, 1]
    for r in range(reqs):
        leaves = jnp.logical_or(first == r, second == r)
        fresh = moved_in[jnp.where(second == r, 1, 0)]
        now = jnp.where(leaves, fresh, cache[r])
        for k in range(n):
            keys[k, r * positions : (r + 1) * positions, :] = now[
                :, k * HEAD_SIZE : (k + 1) * HEAD_SIZE
            ]
            values[k, r * positions : (r + 1) * positions, :] = now[
                :, kv_width + k * HEAD_SIZE : kv_width + (k + 1) * HEAD_SIZE
            ]

    wk_copy.wait()
    key_new = jnp.dot(normed[...], wk[...], preferred_element_type=f32).astype(bf16)
    key_new = rotated(key_new.astype(f32))
    wv_copy.wait()
    value_new = jnp.dot(normed[...], wv[...], preferred_element_type=f32).astype(bf16)

    def page_of(index):
        page = table_ref[adapter_ref[index]]
        return jnp.clip(page - inst * store, 0, store - 1), page // store == inst

    down_copy.wait()
    up_copy.wait()
    for r in range(reqs):
        local, _ = page_of(other * reqs + r)
        down_out[r] = down[local]
        up_out[r] = up[local]
    down_pair = pair(down_out, down_in, 1)
    up_pair = pair(up_out, up_in, 2)
    down_pair.start()
    up_pair.start()

    chunk_rows = chunk_heads * rows
    wide = (chunk_rows, reqs * positions)
    row = lax.broadcasted_iota(jnp.int32, wide, 0)
    column = lax.broadcasted_iota(jnp.int32, wide, 1)
    request = column // positions
    at = me * positions + (column & (positions - 1))
    valid = (request == (row & (reqs - 1))) & (at < by_request(request, own_lengths))
    stat_lane = lax.broadcasted_iota(jnp.int32, (chunk_rows, 128), 1)

    def attend(query, key, value, mask):
        score = lax.dot_general(
            query, key, (((1,), (1,)), ((), ())), preferred_element_type=f32
        )
        score = jnp.where(mask, score * inverse, NEGATIVE)
        top = jnp.max(score, axis=-1, keepdims=True)
        weight = jnp.where(mask, jnp.exp(score - top), 0.0)
        total = jnp.sum(weight, axis=-1, keepdims=True)
        mixed = jnp.dot(weight.astype(bf16), value, preferred_element_type=f32)
        total = jnp.where(total > 0.0, total, 1.0)
        return mixed / total, top + jnp.log(total)

    def part_copy(c, owner, p):
        return pltpu.make_async_remote_copy(
            src_ref=part_out.at[c, p],
            dst_ref=part_in.at[c, owner],
            send_sem=part_send.at[c, p],
            recv_sem=part_recv.at[c, owner],
            device_id={"tp": p},
            device_id_type=MESH,
        )

    stat[...] = jnp.zeros_like(stat)
    for c in range(chunks):

        def one_head(p):
            mixed, level = attend(query_all[c, p], keys[p], values[p], valid)
            at = pl.ds(c * chunk_rows, chunk_rows)
            stat[at, :] = jnp.where(stat_lane == p, level, stat[at, :])
            return mixed.astype(bf16)

        def peer_head(p):
            query_copy(c, p, p).wait_recv()
            part_out[c, p] = one_head(p)
            part_copy(c, me, p).start()

        each_peer(peer_head)
        part_in[c, me] = one_head(me)

    def stat_copy(owner, p):
        return pltpu.make_async_remote_copy(
            src_ref=stat_out.at[p],
            dst_ref=stat_in.at[owner],
            send_sem=stat_send.at[p],
            recv_sem=stat_recv.at[owner],
            device_id={"tp": p},
            device_id_type=MESH,
        )

    turned = jnp.transpose(stat[...])
    for p in range(n):
        stat_out[p] = jnp.broadcast_to(turned[p : p + 1, :], (8, 128))
    stat_in[me] = stat_out[me]
    each_peer(lambda p: stat_copy(me, p).start())

    small = (chunk_rows, rows)
    row = lax.broadcasted_iota(jnp.int32, small, 0)
    column = lax.broadcasted_iota(jnp.int32, small, 1)
    causal = ((row & (reqs - 1)) == (column & (reqs - 1))) & (
        column // reqs <= (row & (rows - 1)) // reqs
    )
    fresh_parts = [attend(query_all[c, me], key_new, value_new, causal) for c in range(chunks)]

    down_pair.wait_recv()
    up_pair.wait_recv()
    for r in range(reqs):
        local, held = page_of(inst * reqs + r)
        down_in[r] = jnp.where(held, down[local], down_in[r])
        up_in[r] = jnp.where(held, up[local], up_in[r])

    each_peer(lambda p: stat_copy(p, p).wait_recv())
    sub = lax.broadcasted_iota(jnp.int32, (8, 128), 0)
    levels = jnp.zeros((8, 128), f32)
    for p in range(n):
        levels = jnp.where(sub == p, stat_in[p], levels)
    levels = jnp.transpose(levels)
    for c in range(chunks):
        each_peer(lambda p: part_copy(c, p, p).wait_recv())
    heads = []
    for c in range(chunks):
        fresh_mixed, fresh_level = fresh_parts[c]
        level = levels[c * chunk_rows : (c + 1) * chunk_rows, :]
        top = jnp.maximum(jnp.max(level, axis=-1, keepdims=True), fresh_level)
        weight = jnp.exp(level - top)
        fresh_weight = jnp.exp(fresh_level - top)
        total = jnp.sum(weight, axis=-1, keepdims=True) + fresh_weight
        mixed = fresh_mixed * fresh_weight
        for p in range(n):
            mixed += part_in[c, p].astype(f32) * weight[:, p : p + 1]
        mixed = (mixed / total).astype(bf16)
        heads += [mixed[h * rows : (h + 1) * rows, :] for h in range(chunk_heads)]
    attended = jnp.concatenate(heads, axis=1)

    def shrink_copy(owner, p):
        return pltpu.make_async_remote_copy(
            src_ref=shrink_part,
            dst_ref=shrink_in.at[owner],
            send_sem=shrink_send.at[p],
            recv_sem=shrink_recv.at[owner],
            device_id={"tp": p},
            device_id_type=MESH,
        )

    row = lax.broadcasted_iota(jnp.int32, (rows, rank), 0) & (reqs - 1)
    shrunk = jnp.zeros((rows, rank), f32)
    for r in range(reqs):
        product = jnp.dot(attended, down_in[r], preferred_element_type=f32)
        shrunk = jnp.where(row == r, product, shrunk)
    shrink_part[...] = shrunk
    each_peer(lambda p: shrink_copy(me, p).start())

    def base_copy(owner, p):
        return pltpu.make_async_remote_copy(
            src_ref=base_out.at[p],
            dst_ref=base_in.at[owner],
            send_sem=base_send.at[p],
            recv_sem=base_recv.at[owner],
            device_id={"tp": p},
            device_id_type=MESH,
        )

    def peer_block(p):
        wo_copy(p).wait()
        base_out[p] = jnp.dot(attended, wo[p], preferred_element_type=f32).astype(bf16)
        base_copy(me, p).start()

    each_peer(peer_block)
    wo_copy(me).wait()
    output = jnp.dot(attended, wo[me], preferred_element_type=f32)

    each_peer(lambda p: shrink_copy(p, p).wait_recv())
    shrink_in[me] = shrink_part[...]
    shrunk = shrink_in[0]
    for p in range(1, n):
        shrunk += shrink_in[p]
    shrunk = shrunk.astype(bf16)
    delta = jnp.zeros((rows, out_cols), f32)
    for r in range(reqs):
        chosen = jnp.where(row == r, shrunk.astype(f32), 0.0).astype(bf16)
        delta += jnp.dot(chosen, up_in[r], preferred_element_type=f32)
    output += ADAPTER_SCALE * delta
    hidden[:, :out_cols] = output

    def add_block(p):
        base_copy(p, p).wait_recv()
        hidden[:, :out_cols] += base_in[p].astype(f32)

    each_peer(add_block)
    for s in range(steps):
        out_ref[s] = hidden[pl.ds(s * reqs, reqs), :out_cols].astype(bf16)

    moving.wait_send()
    down_pair.wait_send()
    up_pair.wait_send()

    def sent(p):
        for c in range(chunks):
            query_copy(c, me, p).wait_send()
            part_copy(c, me, p).wait_send()
        stat_copy(me, p).wait_send()
        shrink_copy(me, p).wait_send()
        base_copy(me, p).wait_send()

    each_peer(sent)


CHUNKS = 2
PIECES = 4


def fused(
    hidden_input,
    input_norm_gain,
    query_weight,
    key_weight,
    value_weight,
    output_weight,
    key_value_cache,
    lengths,
    leaving,
    request_adapter_index,
    adapter_page_table,
    adapter_down_pages,
    adapter_up_pages,
):
    n = lax.axis_size("tp")
    steps, reqs, width = hidden_input.shape
    head_cols = query_weight.shape[1]
    positions, kv_both = key_value_cache.shape[1:]
    store, _, rank = adapter_down_pages.shape
    out_cols = adapter_up_pages.shape[2]
    rows = steps * reqs
    chunk_rows = head_cols // HEAD_SIZE // CHUNKS * rows
    dims = (n, steps, reqs, width, head_cols, positions, store, rank, out_cols, CHUNKS, PIECES)
    bf16, f32 = jnp.bfloat16, jnp.float32
    dma = pltpu.SemaphoreType.DMA
    vmem = pl.BlockSpec(memory_space=pltpu.VMEM)
    smem = pl.BlockSpec(memory_space=pltpu.SMEM)
    hbm = pl.BlockSpec(memory_space=pl.ANY)
    return pl.pallas_call(
        functools.partial(fused_kernel, dims),
        out_shape=jax.ShapeDtypeStruct((steps, reqs, out_cols), bf16),
        in_specs=[vmem, vmem, hbm, hbm, hbm, hbm, hbm, smem, smem, smem, smem, hbm, hbm],
        out_specs=vmem,
        scratch_shapes=[
            pltpu.VMEM((width, head_cols), bf16),
            pltpu.VMEM((width, HEAD_SIZE), bf16),
            pltpu.VMEM((width, HEAD_SIZE), bf16),
            pltpu.VMEM((n, head_cols, out_cols), bf16),
            pltpu.VMEM((reqs, positions, kv_both), bf16),
            pltpu.VMEM((2, positions, kv_both), bf16),
            pltpu.VMEM((2, positions, kv_both), bf16),
            pltpu.VMEM((n, reqs * positions, HEAD_SIZE), bf16),
            pltpu.VMEM((n, reqs * positions, HEAD_SIZE), bf16),
            pltpu.VMEM((store, head_cols, rank), bf16),
            pltpu.VMEM((store, rank, out_cols), bf16),
            pltpu.VMEM((reqs, head_cols, rank), bf16),
            pltpu.VMEM((reqs, rank, out_cols), bf16),
            pltpu.VMEM((reqs, head_cols, rank), bf16),
            pltpu.VMEM((reqs, rank, out_cols), bf16),
            pltpu.VMEM((rows, width), f32),
            pltpu.VMEM((rows, width), bf16),
            pltpu.VMEM((CHUNKS, n, chunk_rows, HEAD_SIZE), bf16),
            pltpu.VMEM((CHUNKS, n, chunk_rows, HEAD_SIZE), bf16),
            pltpu.VMEM((CHUNKS, n, chunk_rows, HEAD_SIZE), bf16),
            pltpu.VMEM((CHUNKS * chunk_rows, 128), f32),
            pltpu.VMEM((n, 8, 128), f32),
            pltpu.VMEM((n, 8, 128), f32),
            pltpu.VMEM((rows, rank), f32),
            pltpu.VMEM((n, rows, rank), f32),
            pltpu.VMEM((n, rows, out_cols), bf16),
            pltpu.VMEM((n, rows, out_cols), bf16),
            dma((CHUNKS, PIECES)),
            dma((2,)),
            dma((n,)),
            dma((3,)),
            dma((3,)),
            dma((3,)),
            dma((CHUNKS, n)),
            dma((CHUNKS, n)),
            dma((CHUNKS, n)),
            dma((CHUNKS, n)),
            dma((n,)),
            dma((n,)),
            dma((n,)),
            dma((n,)),
            dma((n,)),
            dma((n,)),
        ],
        compiler_params=pltpu.CompilerParams(
            collective_id=0, has_side_effects=True, vmem_limit_bytes=60 * 1024 * 1024
        ),
        name="fused",
    )(
        hidden_input,
        input_norm_gain.reshape(1, width),
        query_weight,
        key_weight,
        value_weight,
        output_weight,
        key_value_cache,
        lengths,
        leaving,
        request_adapter_index,
        adapter_page_table,
        adapter_down_pages,
        adapter_up_pages,
    )


def solution(mesh):
    body = fused if mesh.shape["tp"] == KVH and mesh.shape["inst"] == 2 else shards
    return jax.shard_map(
        body,
        mesh=mesh,
        in_specs=(
            P(None, ("groups", "inst"), None),
            P(),
            P(None, "tp"),
            P(None, "tp"),
            P(None, "tp"),
            P("tp", None),
            P(("groups", "inst"), "tp", None),
            P("groups"),
            P("groups", None),
            P("groups"),
            P(),
            P("inst", "tp", None),
            P("inst", None, "tp"),
        ),
        out_specs=P(None, ("groups", "inst"), "tp"),
        check_vma=False,
    )
```

```python
import functools
import math

import jax
import jax.numpy as jnp
from jax import lax
from jax.experimental import pallas as pl
from jax.experimental.pallas import tpu as pltpu
from jax.sharding import PartitionSpec as P

QUERY_HEADS = 64
KVH = 8
HEAD_SIZE = 128
MESH = pl.DeviceIdType.MESH


THETA = 500000.0
ADAPTER_SCALE = 0.5
NEGATIVE = -1e30


def partner(block, axis, bit):
    count = lax.axis_size(axis)
    route = []
    for low in range(count):
        high = low | 1 << bit
        if high != low and high < count:
            route += [(low, high), (high, low)]
    return lax.ppermute(block, axis, route)


def combined_all(value, axis, combine):
    everything = jax.tree.map(
        lambda part, kind: lax.all_gather(part.astype(kind), axis),
        value,
        (jnp.bfloat16, jnp.bfloat16, jnp.bfloat16),
    )

    def take(k):
        return jax.tree.map(lambda part, own: part[k].astype(own.dtype), everything, value)

    return lax.fori_loop(
        1, lax.axis_size(axis), lambda k, so_far: combine(so_far, take(k)), take(0)
    )


def normalize(hidden, input_norm_gain):
    values = hidden.astype(jnp.float32)
    factor = lax.rsqrt(jnp.mean(values * values, axis=-1, keepdims=True) + 1e-05)
    return (values * factor * input_norm_gain.astype(jnp.float32)).astype(jnp.bfloat16)


def rotate(tensor, position):
    middle = tensor.shape[-1] // 2
    freqs = jnp.exp(
        jnp.arange(middle, dtype=jnp.float32) * (-2.0 * math.log(THETA) / tensor.shape[-1])
    )
    angles = position[..., None] * freqs
    cosine = jnp.cos(angles)
    sine_part = jnp.sin(angles)
    first = tensor[..., :middle]
    second = tensor[..., middle:]
    return jnp.concatenate(
        [first * cosine - second * sine_part, second * cosine + first * sine_part], axis=-1
    )


def combine(earlier, later):
    top_first, total_first, mixed_first = earlier
    top_second, total_second, mixed_second = later
    top = jnp.maximum(top_first, top_second)
    scale_first = jnp.exp(top_first - top)
    scale_second = jnp.exp(top_second - top)
    total = total_first * scale_first + total_second * scale_second
    mixed = mixed_first * scale_first[..., None] + mixed_second * scale_second[..., None]
    return (top, total, mixed)


def shards(
    hidden_input,
    input_norm_gain,
    query_weight,
    key_weight,
    value_weight,
    output_weight,
    key_value_cache,
    lengths,
    leaving,
    request_adapter_index,
    adapter_page_table,
    adapter_down_pages,
    adapter_up_pages,
):
    decode_steps, request_rows, width = hidden_input.shape
    device = lax.axis_index("tp")
    instance = lax.axis_index("inst")
    head_cols = query_weight.shape[1]
    local_heads = head_cols // HEAD_SIZE
    positions = key_value_cache.shape[1]
    kv_width = KVH * HEAD_SIZE
    group = QUERY_HEADS // KVH
    normed = normalize(hidden_input, input_norm_gain).reshape(decode_steps * request_rows, width)
    query_part = jnp.dot(normed, query_weight, preferred_element_type=jnp.float32).astype(
        jnp.bfloat16
    )
    key_part = jnp.dot(normed, key_weight, preferred_element_type=jnp.float32).astype(jnp.bfloat16)
    value_part = jnp.dot(normed, value_weight, preferred_element_type=jnp.float32).astype(
        jnp.bfloat16
    )
    query_all, key_all, value_all = (
        lax.all_gather(query_part, "tp", axis=1, tiled=True),
        lax.all_gather(key_part, "tp", axis=1, tiled=True),
        lax.all_gather(value_part, "tp", axis=1, tiled=True),
    )
    lengths_here = lax.dynamic_slice_in_dim(lengths, instance * request_rows, request_rows)
    new_pos = (lengths_here[None, :] + jnp.arange(decode_steps, dtype=jnp.int32)[:, None]).astype(
        jnp.float32
    )[:, :, None]
    query_rot = rotate(
        query_all.reshape(decode_steps, request_rows, QUERY_HEADS, HEAD_SIZE).astype(jnp.float32),
        new_pos,
    ).astype(jnp.bfloat16)
    query_rot = query_rot.reshape(decode_steps, request_rows, KVH, group, HEAD_SIZE)
    key_rot = rotate(
        key_all.reshape(decode_steps, request_rows, KVH, HEAD_SIZE).astype(jnp.float32), new_pos
    ).astype(jnp.bfloat16)
    value_new = value_all.reshape(decode_steps, request_rows, KVH, HEAD_SIZE)
    outgoing_slots = lax.dynamic_index_in_dim(leaving, instance, 0, keepdims=False)
    arriving = partner(key_value_cache[outgoing_slots], "inst", 0)
    cache_now = key_value_cache.at[outgoing_slots].set(arriving)
    pages = adapter_page_table[request_adapter_index]
    adapter_store_size = adapter_down_pages.shape[0]
    own_pages = lax.dynamic_slice_in_dim(pages, instance * request_rows, request_rows)
    partner_pages = lax.dynamic_slice_in_dim(pages, (1 - instance) * request_rows, request_rows)

    def select_pages(wanted):
        local_page_index = jnp.clip(
            wanted - instance * adapter_store_size, 0, adapter_store_size - 1
        )
        down_matrix_flat = adapter_down_pages[local_page_index].reshape(request_rows, -1)
        up_matrix_flat = adapter_up_pages[local_page_index].reshape(request_rows, -1)
        return (
            jnp.concatenate([down_matrix_flat, up_matrix_flat], axis=1),
            wanted // adapter_store_size == instance,
        )

    outgoing_pages, held_there = select_pages(partner_pages)
    outgoing_pages = jnp.where(held_there[:, None], outgoing_pages, jnp.zeros_like(outgoing_pages))
    arriving_pages = partner(outgoing_pages, "inst", 0)
    local_pages, held_here = select_pages(own_pages)
    fetched_pages = jnp.where(held_here[:, None], local_pages, arriving_pages)
    down_matrix_size = adapter_down_pages.shape[1] * adapter_down_pages.shape[2]
    down_matrix_rows = fetched_pages[:, :down_matrix_size].reshape(
        request_rows, adapter_down_pages.shape[1], adapter_down_pages.shape[2]
    )
    up_matrix_rows = fetched_pages[:, down_matrix_size:].reshape(
        request_rows, adapter_up_pages.shape[1], adapter_up_pages.shape[2]
    )
    keys = cache_now[:, :, :kv_width].reshape(request_rows, positions, KVH, HEAD_SIZE)
    values = cache_now[:, :, kv_width:].reshape(request_rows, positions, KVH, HEAD_SIZE)
    place = device * positions + jnp.arange(positions, dtype=jnp.int32)
    valid = place[None, :] < lengths_here[:, None]
    valid_b = valid[None, :, None, None, :]
    inverse = 1.0 / math.sqrt(HEAD_SIZE)
    cache_scores = (
        jnp.einsum("srkgd,rpkd->srkgp", query_rot, keys, preferred_element_type=jnp.float32)
        * inverse
    )
    cache_scores = jnp.where(valid_b, cache_scores, NEGATIVE)
    new_scores = (
        jnp.einsum("srkgd,trkd->srkgt", query_rot, key_rot, preferred_element_type=jnp.float32)
        * inverse
    )
    causal = (jnp.arange(decode_steps)[None, :] <= jnp.arange(decode_steps)[:, None]) & (
        device == 0
    )
    causal_b = causal[:, None, None, None, :]
    new_scores = jnp.where(causal_b, new_scores, NEGATIVE)
    top = jnp.maximum(cache_scores.max(-1), new_scores.max(-1))
    cache_weights = jnp.exp(cache_scores - top[..., None]) * valid_b.astype(jnp.float32)
    new_weights = jnp.exp(new_scores - top[..., None]) * causal_b.astype(jnp.float32)
    total = cache_weights.sum(-1) + new_weights.sum(-1)
    mixed = jnp.einsum(
        "srkgp,rpkd->srkgd",
        cache_weights.astype(jnp.bfloat16),
        values,
        preferred_element_type=jnp.float32,
    )
    mixed = mixed + jnp.einsum(
        "srkgt,trkd->srkgd",
        new_weights.astype(jnp.bfloat16),
        value_new,
        preferred_element_type=jnp.float32,
    )
    top = top.reshape(decode_steps, request_rows, QUERY_HEADS)
    total = total.reshape(decode_steps, request_rows, QUERY_HEADS)
    mixed = mixed.reshape(decode_steps, request_rows, QUERY_HEADS, HEAD_SIZE)
    top_all, total_all, mixed_all = combined_all((top, total, mixed), "tp", combine)
    first_head = device * local_heads
    total_own = lax.dynamic_slice_in_dim(total_all, first_head, local_heads, 2)
    mixed_own = lax.dynamic_slice_in_dim(mixed_all, first_head, local_heads, 2)
    attention_output = mixed_own / total_own[..., None]
    attention_output = attention_output.astype(jnp.bfloat16).reshape(
        decode_steps * request_rows, head_cols
    )
    base_part = jnp.dot(attention_output, output_weight, preferred_element_type=jnp.float32)
    shrink_part = jnp.einsum(
        "src,rck->srk",
        attention_output.reshape(decode_steps, request_rows, head_cols),
        down_matrix_rows,
        preferred_element_type=jnp.float32,
    )
    shrunk_output = lax.psum(shrink_part, "tp")
    base_output = lax.psum_scatter(
        base_part.astype(jnp.bfloat16), "tp", scatter_dimension=1, tiled=True
    ).astype(jnp.float32)
    shrunk_output = shrunk_output.astype(jnp.bfloat16)
    adapter_delta = jnp.einsum(
        "srk,rkd->srd", shrunk_output, up_matrix_rows, preferred_element_type=jnp.float32
    )
    return (
        base_output.reshape(decode_steps, request_rows, -1) + ADAPTER_SCALE * adapter_delta
    ).astype(jnp.bfloat16)


def fused_kernel(
    dims,
    hidden_ref,
    gain_ref,
    wq_hbm,
    wk_hbm,
    wv_hbm,
    wo_hbm,
    cache_hbm,
    lengths_ref,
    leaving_ref,
    adapter_ref,
    table_ref,
    down_hbm,
    up_hbm,
    out_ref,
    wq,
    wk,
    wv,
    wo,
    cache,
    moved_out,
    moved_in,
    keys,
    values,
    down,
    up,
    down_out,
    up_out,
    down_in,
    up_in,
    hidden,
    normed,
    query_all,
    part_out,
    part_in,
    stat,
    stat_out,
    stat_in,
    shrink_part,
    shrink_in,
    base_out,
    base_in,
    wq_sem,
    wkv_sem,
    wo_sem,
    store_sem,
    pair_send,
    pair_recv,
    query_send,
    query_recv,
    part_send,
    part_recv,
    stat_send,
    stat_recv,
    shrink_send,
    shrink_recv,
    base_send,
    base_recv,
):
    n, steps, reqs, width, head_cols, positions, store, rank, out_cols, chunks, pieces = dims
    rows = steps * reqs
    head_count = head_cols // HEAD_SIZE
    chunk_heads = head_count // chunks
    chunk_cols = chunk_heads * HEAD_SIZE
    piece = width // pieces
    kv_width = n * HEAD_SIZE
    me = lax.axis_index("tp")
    inst = lax.axis_index("inst")
    other = 1 - inst
    f32, bf16 = jnp.float32, jnp.bfloat16
    inverse = 1.0 / math.sqrt(HEAD_SIZE)

    def each_peer(body):
        def step(o, carry):
            body(lax.rem(me + 1 + o, n))
            return carry

        lax.fori_loop(0, n - 1, step, 0)

    cache_copy = pltpu.make_async_copy(cache_hbm, cache, store_sem.at[0])
    cache_copy.start()
    wq_copies = {}
    for c in range(chunks):
        for k in range(pieces):
            at = (pl.ds(k * piece, piece), pl.ds(c * chunk_cols, chunk_cols))
            wq_copies[c, k] = pltpu.make_async_copy(
                wq_hbm.at[at], wq.at[at], wq_sem.at[c, k]
            )
            wq_copies[c, k].start()
    wk_copy = pltpu.make_async_copy(wk_hbm, wk, wkv_sem.at[0])
    wv_copy = pltpu.make_async_copy(wv_hbm, wv, wkv_sem.at[1])
    down_copy = pltpu.make_async_copy(down_hbm, down, store_sem.at[1])
    up_copy = pltpu.make_async_copy(up_hbm, up, store_sem.at[2])
    wk_copy.start()
    wv_copy.start()
    down_copy.start()
    up_copy.start()

    def wo_copy(p):
        cols = pl.ds(pl.multiple_of(p * out_cols, out_cols), out_cols)
        return pltpu.make_async_copy(wo_hbm.at[:, cols], wo.at[p], wo_sem.at[p])

    def start_wo(o, carry):
        wo_copy(lax.rem(me + 1 + o, n)).start()
        return carry

    lax.fori_loop(0, n, start_wo, 0)

    barrier = pltpu.get_barrier_semaphore()
    each_peer(lambda p: pl.semaphore_signal(barrier, inc=1, device_id={"tp": p}, device_id_type=MESH))
    pl.semaphore_signal(barrier, inc=1, device_id={"inst": other}, device_id_type=MESH)

    for s in range(steps):
        hidden[pl.ds(s * reqs, reqs), :] = hidden_ref[s].astype(f32)
    block = hidden[...]
    factor = lax.rsqrt(jnp.mean(block * block, axis=-1, keepdims=True) + 1e-05)
    gain = gain_ref[...].astype(f32)
    for i in range(width // 128):
        cols = slice(i * 128, (i + 1) * 128)
        normed[:, cols] = (hidden[:, cols] * factor * gain[i : i + 1, :]).astype(bf16)

    own_lengths = [lengths_ref[inst * reqs + r] for r in range(reqs)]

    def by_request(index, numbers):
        chosen = jnp.full(index.shape, numbers[0], jnp.int32)
        for r in range(1, reqs):
            chosen = jnp.where(index == r, numbers[r], chosen)
        return chosen

    row = lax.broadcasted_iota(jnp.int32, (rows, HEAD_SIZE), 0)
    lane = lax.broadcasted_iota(jnp.int32, (rows, HEAD_SIZE), 1)
    half = HEAD_SIZE // 2
    place = (by_request(row & (reqs - 1), own_lengths) + row // reqs).astype(f32)
    freqs = jnp.exp((lane & (half - 1)).astype(f32) * (-2.0 * math.log(THETA) / HEAD_SIZE))
    angle = place * freqs
    cosine = jnp.cos(angle)
    sine = jnp.where(lane < half, -1.0, 1.0) * jnp.sin(angle)

    def rotated(tensor):
        return (tensor * cosine + pltpu.roll(tensor, half, 1) * sine).astype(bf16)

    cache_copy.wait()
    for j in range(2):
        moved_out[j] = cache[leaving_ref[inst, j]]

    def pair(src, dst, k):
        return pltpu.make_async_remote_copy(
            src_ref=src,
            dst_ref=dst,
            send_sem=pair_send.at[k],
            recv_sem=pair_recv.at[k],
            device_id={"inst": other},
            device_id_type=MESH,
        )

    moving = pair(moved_out, moved_in, 0)

    def query_copy(c, owner, p):
        return pltpu.make_async_remote_copy(
            src_ref=query_all.at[c, owner],
            dst_ref=query_all.at[c, owner],
            send_sem=query_send.at[c, p],
            recv_sem=query_recv.at[c, owner],
            device_id={"tp": p},
            device_id_type=MESH,
        )

    for c in range(chunks):
        total = jnp.zeros((rows, chunk_cols), f32)
        for k in range(pieces):
            wq_copies[c, k].wait()
            total += jnp.dot(
                normed[:, k * piece : (k + 1) * piece],
                wq[k * piece : (k + 1) * piece, c * chunk_cols : (c + 1) * chunk_cols],
                preferred_element_type=f32,
            )
        total = total.astype(bf16).astype(f32)
        for h in range(chunk_heads):
            query_all[c, me, h * rows : (h + 1) * rows, :] = rotated(
                total[:, h * HEAD_SIZE : (h + 1) * HEAD_SIZE]
            )
        if c == 0:
            pl.semaphore_wait(barrier, n)
            moving.start()
        each_peer(lambda p: query_copy(c, me, p).start())

    moving.wait_recv()
    first, second = leaving_ref[inst, 0], leaving_ref[inst, 1]
    for r in range(reqs):
        leaves = jnp.logical_or(first == r, second == r)
        fresh = moved_in[jnp.where(second == r, 1, 0)]
        now = jnp.where(leaves, fresh, cache[r])
        for k in range(n):
            keys[k, r * positions : (r + 1) * positions, :] = now[
                :, k * HEAD_SIZE : (k + 1) * HEAD_SIZE
            ]
            values[k, r * positions : (r + 1) * positions, :] = now[
                :, kv_width + k * HEAD_SIZE : kv_width + (k + 1) * HEAD_SIZE
            ]

    wk_copy.wait()
    key_new = jnp.dot(normed[...], wk[...], preferred_element_type=f32).astype(bf16)
    key_new = rotated(key_new.astype(f32))
    wv_copy.wait()
    value_new = jnp.dot(normed[...], wv[...], preferred_element_type=f32).astype(bf16)

    def page_of(index):
        page = table_ref[adapter_ref[index]]
        return jnp.clip(page - inst * store, 0, store - 1), page // store == inst

    down_copy.wait()
    up_copy.wait()
    for r in range(reqs):
        local, _ = page_of(other * reqs + r)
        down_out[r] = down[local]
        up_out[r] = up[local]
    down_pair = pair(down_out, down_in, 1)
    up_pair = pair(up_out, up_in, 2)
    down_pair.start()
    up_pair.start()

    chunk_rows = chunk_heads * rows
    wide = (chunk_rows, reqs * positions)
    row = lax.broadcasted_iota(jnp.int32, wide, 0)
    column = lax.broadcasted_iota(jnp.int32, wide, 1)
    request = column // positions
    at = me * positions + (column & (positions - 1))
    valid = (request == (row & (reqs - 1))) & (at < by_request(request, own_lengths))
    stat_lane = lax.broadcasted_iota(jnp.int32, (chunk_rows, 128), 1)

    def attend(query, key, value, mask):
        score = lax.dot_general(
            query, key, (((1,), (1,)), ((), ())), preferred_element_type=f32
        )
        score = jnp.where(mask, score * inverse, NEGATIVE)
        top = jnp.max(score, axis=-1, keepdims=True)
        weight = jnp.where(mask, jnp.exp(score - top), 0.0)
        total = jnp.sum(weight, axis=-1, keepdims=True)
        mixed = jnp.dot(weight.astype(bf16), value, preferred_element_type=f32)
        total = jnp.where(total > 0.0, total, 1.0)
        return mixed / total, top + jnp.log(total)

    def part_copy(c, owner, p):
        return pltpu.make_async_remote_copy(
            src_ref=part_out.at[c, p],
            dst_ref=part_in.at[c, owner],
            send_sem=part_send.at[c, p],
            recv_sem=part_recv.at[c, owner],
            device_id={"tp": p},
            device_id_type=MESH,
        )

    for c in range(chunks):
        levels = jnp.zeros((chunk_rows, 128), f32)
        for begin in range(0, n, 4):
            some = [lax.rem(me + o, n) for o in range(begin, begin + 4)]
            for p in some:
                if p is not some[0] or begin > 0:
                    query_copy(c, p, p).wait_recv()
            mixed = [attend(query_all[c, p], keys[p], values[p], valid) for p in some]
            for p, (part, level) in zip(some, mixed):
                levels = jnp.where(stat_lane == p, level, levels)
                if p is not some[0] or begin > 0:
                    part_out[c, p] = part.astype(bf16)
                    part_copy(c, me, p).start()
                else:
                    part_in[c, me] = part.astype(bf16)
        stat[c * chunk_rows : (c + 1) * chunk_rows, :] = levels

    def stat_copy(owner, p):
        return pltpu.make_async_remote_copy(
            src_ref=stat_out.at[p],
            dst_ref=stat_in.at[owner],
            send_sem=stat_send.at[p],
            recv_sem=stat_recv.at[owner],
            device_id={"tp": p},
            device_id_type=MESH,
        )

    turned = jnp.transpose(stat[...])
    for p in range(n):
        stat_out[p] = jnp.broadcast_to(turned[p : p + 1, :], (8, 128))
    stat_in[me] = stat_out[me]
    each_peer(lambda p: stat_copy(me, p).start())

    small = (chunk_rows, rows)
    row = lax.broadcasted_iota(jnp.int32, small, 0)
    column = lax.broadcasted_iota(jnp.int32, small, 1)
    causal = ((row & (reqs - 1)) == (column & (reqs - 1))) & (
        column // reqs <= (row & (rows - 1)) // reqs
    )
    fresh_parts = [attend(query_all[c, me], key_new, value_new, causal) for c in range(chunks)]

    down_pair.wait_recv()
    up_pair.wait_recv()
    for r in range(reqs):
        local, held = page_of(inst * reqs + r)
        down_in[r] = jnp.where(held, down[local], down_in[r])
        up_in[r] = jnp.where(held, up[local], up_in[r])

    each_peer(lambda p: stat_copy(p, p).wait_recv())
    sub = lax.broadcasted_iota(jnp.int32, (8, 128), 0)
    levels = jnp.zeros((8, 128), f32)
    for p in range(n):
        levels = jnp.where(sub == p, stat_in[p], levels)
    levels = jnp.transpose(levels)
    for c in range(chunks):
        each_peer(lambda p: part_copy(c, p, p).wait_recv())
    heads = []
    for c in range(chunks):
        fresh_mixed, fresh_level = fresh_parts[c]
        level = levels[c * chunk_rows : (c + 1) * chunk_rows, :]
        top = jnp.maximum(jnp.max(level, axis=-1, keepdims=True), fresh_level)
        weight = jnp.exp(level - top)
        fresh_weight = jnp.exp(fresh_level - top)
        total = jnp.sum(weight, axis=-1, keepdims=True) + fresh_weight
        mixed = fresh_mixed * fresh_weight
        for p in range(n):
            mixed += part_in[c, p].astype(f32) * weight[:, p : p + 1]
        mixed = (mixed / total).astype(bf16)
        heads += [mixed[h * rows : (h + 1) * rows, :] for h in range(chunk_heads)]
    attended = jnp.concatenate(heads, axis=1)

    def shrink_copy(owner, p):
        return pltpu.make_async_remote_copy(
            src_ref=shrink_part,
            dst_ref=shrink_in.at[owner],
            send_sem=shrink_send.at[p],
            recv_sem=shrink_recv.at[owner],
            device_id={"tp": p},
            device_id_type=MESH,
        )

    row = lax.broadcasted_iota(jnp.int32, (rows, rank), 0) & (reqs - 1)
    shrunk = jnp.zeros((rows, rank), f32)
    for r in range(reqs):
        product = lax.dot_general(
            attended, down_in[r], (((1,), (1,)), ((), ())), preferred_element_type=f32
        )
        shrunk = jnp.where(row == r, product, shrunk)
    shrink_part[...] = shrunk
    each_peer(lambda p: shrink_copy(me, p).start())

    def base_copy(owner, p):
        return pltpu.make_async_remote_copy(
            src_ref=base_out.at[p],
            dst_ref=base_in.at[owner],
            send_sem=base_send.at[p],
            recv_sem=base_recv.at[owner],
            device_id={"tp": p},
            device_id_type=MESH,
        )

    def peer_block(p):
        wo_copy(p).wait()
        base_out[p] = jnp.dot(attended, wo[p], preferred_element_type=f32).astype(bf16)
        base_copy(me, p).start()

    each_peer(peer_block)
    wo_copy(me).wait()
    output = jnp.dot(attended, wo[me], preferred_element_type=f32)

    each_peer(lambda p: shrink_copy(p, p).wait_recv())
    shrink_in[me] = shrink_part[...]
    shrunk = shrink_in[0]
    for p in range(1, n):
        shrunk += shrink_in[p]
    shrunk = shrunk.astype(bf16)
    delta = jnp.zeros((rows, out_cols), f32)
    for r in range(reqs):
        chosen = jnp.where(row == r, shrunk.astype(f32), 0.0).astype(bf16)
        delta += jnp.dot(chosen, up_in[r], preferred_element_type=f32)
    output += ADAPTER_SCALE * delta
    each_peer(lambda p: base_copy(p, p).wait_recv())
    base_in[me] = jnp.zeros((rows, out_cols), bf16)
    for p in range(n):
        output += base_in[p].astype(f32)
    hidden[:, :out_cols] = output
    for s in range(steps):
        out_ref[s] = hidden[pl.ds(s * reqs, reqs), :out_cols].astype(bf16)

    moving.wait_send()
    down_pair.wait_send()
    up_pair.wait_send()

    def sent(p):
        for c in range(chunks):
            query_copy(c, me, p).wait_send()
            part_copy(c, me, p).wait_send()
        stat_copy(me, p).wait_send()
        shrink_copy(me, p).wait_send()
        base_copy(me, p).wait_send()

    each_peer(sent)


CHUNKS = 2
PIECES = 4


def fused(
    hidden_input,
    input_norm_gain,
    query_weight,
    key_weight,
    value_weight,
    output_weight,
    key_value_cache,
    lengths,
    leaving,
    request_adapter_index,
    adapter_page_table,
    adapter_down_pages,
    adapter_up_pages,
):
    n = lax.axis_size("tp")
    steps, reqs, width = hidden_input.shape
    head_cols = query_weight.shape[1]
    positions, kv_both = key_value_cache.shape[1:]
    store, _, rank = adapter_down_pages.shape
    out_cols = adapter_up_pages.shape[2]
    rows = steps * reqs
    chunk_rows = head_cols // HEAD_SIZE // CHUNKS * rows
    dims = (n, steps, reqs, width, head_cols, positions, store, rank, out_cols, CHUNKS, PIECES)
    bf16, f32 = jnp.bfloat16, jnp.float32
    dma = pltpu.SemaphoreType.DMA
    vmem = pl.BlockSpec(memory_space=pltpu.VMEM)
    smem = pl.BlockSpec(memory_space=pltpu.SMEM)
    hbm = pl.BlockSpec(memory_space=pl.ANY)
    return pl.pallas_call(
        functools.partial(fused_kernel, dims),
        out_shape=jax.ShapeDtypeStruct((steps, reqs, out_cols), bf16),
        in_specs=[vmem, vmem, hbm, hbm, hbm, hbm, hbm, smem, smem, smem, smem, hbm, hbm],
        out_specs=vmem,
        scratch_shapes=[
            pltpu.VMEM((width, head_cols), bf16),
            pltpu.VMEM((width, HEAD_SIZE), bf16),
            pltpu.VMEM((width, HEAD_SIZE), bf16),
            pltpu.VMEM((n, head_cols, out_cols), bf16),
            pltpu.VMEM((reqs, positions, kv_both), bf16),
            pltpu.VMEM((2, positions, kv_both), bf16),
            pltpu.VMEM((2, positions, kv_both), bf16),
            pltpu.VMEM((n, reqs * positions, HEAD_SIZE), bf16),
            pltpu.VMEM((n, reqs * positions, HEAD_SIZE), bf16),
            pltpu.VMEM((store, rank, head_cols), bf16),
            pltpu.VMEM((store, rank, out_cols), bf16),
            pltpu.VMEM((reqs, rank, head_cols), bf16),
            pltpu.VMEM((reqs, rank, out_cols), bf16),
            pltpu.VMEM((reqs, rank, head_cols), bf16),
            pltpu.VMEM((reqs, rank, out_cols), bf16),
            pltpu.VMEM((rows, width), f32),
            pltpu.VMEM((rows, width), bf16),
            pltpu.VMEM((CHUNKS, n, chunk_rows, HEAD_SIZE), bf16),
            pltpu.VMEM((CHUNKS, n, chunk_rows, HEAD_SIZE), bf16),
            pltpu.VMEM((CHUNKS, n, chunk_rows, HEAD_SIZE), bf16),
            pltpu.VMEM((CHUNKS * chunk_rows, 128), f32),
            pltpu.VMEM((n, 8, 128), f32),
            pltpu.VMEM((n, 8, 128), f32),
            pltpu.VMEM((rows, rank), f32),
            pltpu.VMEM((n, rows, rank), f32),
            pltpu.VMEM((n, rows, out_cols), bf16),
            pltpu.VMEM((n, rows, out_cols), bf16),
            dma((CHUNKS, PIECES)),
            dma((2,)),
            dma((n,)),
            dma((3,)),
            dma((3,)),
            dma((3,)),
            dma((CHUNKS, n)),
            dma((CHUNKS, n)),
            dma((CHUNKS, n)),
            dma((CHUNKS, n)),
            dma((n,)),
            dma((n,)),
            dma((n,)),
            dma((n,)),
            dma((n,)),
            dma((n,)),
        ],
        compiler_params=pltpu.CompilerParams(
            collective_id=0, has_side_effects=True, vmem_limit_bytes=60 * 1024 * 1024
        ),
        name="fused",
    )(
        hidden_input,
        input_norm_gain.reshape(width // 128, 128),
        query_weight,
        key_weight,
        value_weight,
        output_weight,
        key_value_cache,
        lengths,
        leaving,
        request_adapter_index,
        adapter_page_table,
        jnp.swapaxes(adapter_down_pages, 1, 2),
        adapter_up_pages,
    )


def solution(mesh):
    body = fused if mesh.shape["tp"] == KVH and mesh.shape["inst"] == 2 else shards
    return jax.shard_map(
        body,
        mesh=mesh,
        in_specs=(
            P(None, ("groups", "inst"), None),
            P(),
            P(None, "tp"),
            P(None, "tp"),
            P(None, "tp"),
            P("tp", None),
            P(("groups", "inst"), "tp", None),
            P("groups"),
            P("groups", None),
            P("groups"),
            P(),
            P("inst", "tp", None),
            P("inst", None, "tp"),
        ),
        out_specs=P(None, ("groups", "inst"), "tp"),
        check_vma=False,
    )
```

```python
import functools
import math

import jax
import jax.numpy as jnp
from jax import lax
from jax.experimental import pallas as pl
from jax.experimental.pallas import tpu as pltpu
from jax.sharding import PartitionSpec as P

QUERY_HEADS = 64
KVH = 8
HEAD_SIZE = 128
MESH = pl.DeviceIdType.MESH


THETA = 500000.0
ADAPTER_SCALE = 0.5
NEGATIVE = -1e30


def partner(block, axis, bit):
    count = lax.axis_size(axis)
    route = []
    for low in range(count):
        high = low | 1 << bit
        if high != low and high < count:
            route += [(low, high), (high, low)]
    return lax.ppermute(block, axis, route)


def combined_all(value, axis, combine):
    everything = jax.tree.map(
        lambda part, kind: lax.all_gather(part.astype(kind), axis),
        value,
        (jnp.bfloat16, jnp.bfloat16, jnp.bfloat16),
    )

    def take(k):
        return jax.tree.map(lambda part, own: part[k].astype(own.dtype), everything, value)

    return lax.fori_loop(
        1, lax.axis_size(axis), lambda k, so_far: combine(so_far, take(k)), take(0)
    )


def normalize(hidden, input_norm_gain):
    values = hidden.astype(jnp.float32)
    factor = lax.rsqrt(jnp.mean(values * values, axis=-1, keepdims=True) + 1e-05)
    return (values * factor * input_norm_gain.astype(jnp.float32)).astype(jnp.bfloat16)


def rotate(tensor, position):
    middle = tensor.shape[-1] // 2
    freqs = jnp.exp(
        jnp.arange(middle, dtype=jnp.float32) * (-2.0 * math.log(THETA) / tensor.shape[-1])
    )
    angles = position[..., None] * freqs
    cosine = jnp.cos(angles)
    sine_part = jnp.sin(angles)
    first = tensor[..., :middle]
    second = tensor[..., middle:]
    return jnp.concatenate(
        [first * cosine - second * sine_part, second * cosine + first * sine_part], axis=-1
    )


def combine(earlier, later):
    top_first, total_first, mixed_first = earlier
    top_second, total_second, mixed_second = later
    top = jnp.maximum(top_first, top_second)
    scale_first = jnp.exp(top_first - top)
    scale_second = jnp.exp(top_second - top)
    total = total_first * scale_first + total_second * scale_second
    mixed = mixed_first * scale_first[..., None] + mixed_second * scale_second[..., None]
    return (top, total, mixed)


def shards(
    hidden_input,
    input_norm_gain,
    query_weight,
    key_weight,
    value_weight,
    output_weight,
    key_value_cache,
    lengths,
    leaving,
    request_adapter_index,
    adapter_page_table,
    adapter_down_pages,
    adapter_up_pages,
):
    decode_steps, request_rows, width = hidden_input.shape
    device = lax.axis_index("tp")
    instance = lax.axis_index("inst")
    head_cols = query_weight.shape[1]
    local_heads = head_cols // HEAD_SIZE
    positions = key_value_cache.shape[1]
    kv_width = KVH * HEAD_SIZE
    group = QUERY_HEADS // KVH
    normed = normalize(hidden_input, input_norm_gain).reshape(decode_steps * request_rows, width)
    query_part = jnp.dot(normed, query_weight, preferred_element_type=jnp.float32).astype(
        jnp.bfloat16
    )
    key_part = jnp.dot(normed, key_weight, preferred_element_type=jnp.float32).astype(jnp.bfloat16)
    value_part = jnp.dot(normed, value_weight, preferred_element_type=jnp.float32).astype(
        jnp.bfloat16
    )
    query_all, key_all, value_all = (
        lax.all_gather(query_part, "tp", axis=1, tiled=True),
        lax.all_gather(key_part, "tp", axis=1, tiled=True),
        lax.all_gather(value_part, "tp", axis=1, tiled=True),
    )
    lengths_here = lax.dynamic_slice_in_dim(lengths, instance * request_rows, request_rows)
    new_pos = (lengths_here[None, :] + jnp.arange(decode_steps, dtype=jnp.int32)[:, None]).astype(
        jnp.float32
    )[:, :, None]
    query_rot = rotate(
        query_all.reshape(decode_steps, request_rows, QUERY_HEADS, HEAD_SIZE).astype(jnp.float32),
        new_pos,
    ).astype(jnp.bfloat16)
    query_rot = query_rot.reshape(decode_steps, request_rows, KVH, group, HEAD_SIZE)
    key_rot = rotate(
        key_all.reshape(decode_steps, request_rows, KVH, HEAD_SIZE).astype(jnp.float32), new_pos
    ).astype(jnp.bfloat16)
    value_new = value_all.reshape(decode_steps, request_rows, KVH, HEAD_SIZE)
    outgoing_slots = lax.dynamic_index_in_dim(leaving, instance, 0, keepdims=False)
    arriving = partner(key_value_cache[outgoing_slots], "inst", 0)
    cache_now = key_value_cache.at[outgoing_slots].set(arriving)
    pages = adapter_page_table[request_adapter_index]
    adapter_store_size = adapter_down_pages.shape[0]
    own_pages = lax.dynamic_slice_in_dim(pages, instance * request_rows, request_rows)
    partner_pages = lax.dynamic_slice_in_dim(pages, (1 - instance) * request_rows, request_rows)

    def select_pages(wanted):
        local_page_index = jnp.clip(
            wanted - instance * adapter_store_size, 0, adapter_store_size - 1
        )
        down_matrix_flat = adapter_down_pages[local_page_index].reshape(request_rows, -1)
        up_matrix_flat = adapter_up_pages[local_page_index].reshape(request_rows, -1)
        return (
            jnp.concatenate([down_matrix_flat, up_matrix_flat], axis=1),
            wanted // adapter_store_size == instance,
        )

    outgoing_pages, held_there = select_pages(partner_pages)
    outgoing_pages = jnp.where(held_there[:, None], outgoing_pages, jnp.zeros_like(outgoing_pages))
    arriving_pages = partner(outgoing_pages, "inst", 0)
    local_pages, held_here = select_pages(own_pages)
    fetched_pages = jnp.where(held_here[:, None], local_pages, arriving_pages)
    down_matrix_size = adapter_down_pages.shape[1] * adapter_down_pages.shape[2]
    down_matrix_rows = fetched_pages[:, :down_matrix_size].reshape(
        request_rows, adapter_down_pages.shape[1], adapter_down_pages.shape[2]
    )
    up_matrix_rows = fetched_pages[:, down_matrix_size:].reshape(
        request_rows, adapter_up_pages.shape[1], adapter_up_pages.shape[2]
    )
    keys = cache_now[:, :, :kv_width].reshape(request_rows, positions, KVH, HEAD_SIZE)
    values = cache_now[:, :, kv_width:].reshape(request_rows, positions, KVH, HEAD_SIZE)
    place = device * positions + jnp.arange(positions, dtype=jnp.int32)
    valid = place[None, :] < lengths_here[:, None]
    valid_b = valid[None, :, None, None, :]
    inverse = 1.0 / math.sqrt(HEAD_SIZE)
    cache_scores = (
        jnp.einsum("srkgd,rpkd->srkgp", query_rot, keys, preferred_element_type=jnp.float32)
        * inverse
    )
    cache_scores = jnp.where(valid_b, cache_scores, NEGATIVE)
    new_scores = (
        jnp.einsum("srkgd,trkd->srkgt", query_rot, key_rot, preferred_element_type=jnp.float32)
        * inverse
    )
    causal = (jnp.arange(decode_steps)[None, :] <= jnp.arange(decode_steps)[:, None]) & (
        device == 0
    )
    causal_b = causal[:, None, None, None, :]
    new_scores = jnp.where(causal_b, new_scores, NEGATIVE)
    top = jnp.maximum(cache_scores.max(-1), new_scores.max(-1))
    cache_weights = jnp.exp(cache_scores - top[..., None]) * valid_b.astype(jnp.float32)
    new_weights = jnp.exp(new_scores - top[..., None]) * causal_b.astype(jnp.float32)
    total = cache_weights.sum(-1) + new_weights.sum(-1)
    mixed = jnp.einsum(
        "srkgp,rpkd->srkgd",
        cache_weights.astype(jnp.bfloat16),
        values,
        preferred_element_type=jnp.float32,
    )
    mixed = mixed + jnp.einsum(
        "srkgt,trkd->srkgd",
        new_weights.astype(jnp.bfloat16),
        value_new,
        preferred_element_type=jnp.float32,
    )
    top = top.reshape(decode_steps, request_rows, QUERY_HEADS)
    total = total.reshape(decode_steps, request_rows, QUERY_HEADS)
    mixed = mixed.reshape(decode_steps, request_rows, QUERY_HEADS, HEAD_SIZE)
    top_all, total_all, mixed_all = combined_all((top, total, mixed), "tp", combine)
    first_head = device * local_heads
    total_own = lax.dynamic_slice_in_dim(total_all, first_head, local_heads, 2)
    mixed_own = lax.dynamic_slice_in_dim(mixed_all, first_head, local_heads, 2)
    attention_output = mixed_own / total_own[..., None]
    attention_output = attention_output.astype(jnp.bfloat16).reshape(
        decode_steps * request_rows, head_cols
    )
    base_part = jnp.dot(attention_output, output_weight, preferred_element_type=jnp.float32)
    shrink_part = jnp.einsum(
        "src,rck->srk",
        attention_output.reshape(decode_steps, request_rows, head_cols),
        down_matrix_rows,
        preferred_element_type=jnp.float32,
    )
    shrunk_output = lax.psum(shrink_part, "tp")
    base_output = lax.psum_scatter(
        base_part.astype(jnp.bfloat16), "tp", scatter_dimension=1, tiled=True
    ).astype(jnp.float32)
    shrunk_output = shrunk_output.astype(jnp.bfloat16)
    adapter_delta = jnp.einsum(
        "srk,rkd->srd", shrunk_output, up_matrix_rows, preferred_element_type=jnp.float32
    )
    return (
        base_output.reshape(decode_steps, request_rows, -1) + ADAPTER_SCALE * adapter_delta
    ).astype(jnp.bfloat16)


def fused_kernel(
    dims,
    hidden_ref,
    gain_ref,
    wq_hbm,
    wk_hbm,
    wv_hbm,
    wo_hbm,
    cache_hbm,
    lengths_ref,
    leaving_ref,
    adapter_ref,
    table_ref,
    down_hbm,
    up_hbm,
    out_ref,
    wq,
    wk,
    wv,
    wo,
    cache,
    moved_out,
    moved_in,
    keys,
    values,
    down,
    up,
    down_out,
    up_out,
    down_in,
    up_in,
    hidden,
    normed,
    query_all,
    part_out,
    part_in,
    shrink_part,
    shrink_in,
    base_out,
    base_in,
    wq_sem,
    wkv_sem,
    wo_sem,
    store_sem,
    pair_send,
    pair_recv,
    query_send,
    query_recv,
    part_send,
    part_recv,
    shrink_send,
    shrink_recv,
    base_send,
    base_recv,
):
    n, steps, reqs, width, head_cols, positions, store, rank, out_cols, chunks, pieces = dims
    rows = steps * reqs
    head_count = head_cols // HEAD_SIZE
    chunk_heads = head_count // chunks
    chunk_cols = chunk_heads * HEAD_SIZE
    piece = width // pieces
    kv_width = n * HEAD_SIZE
    me = lax.axis_index("tp")
    inst = lax.axis_index("inst")
    other = 1 - inst
    f32, bf16 = jnp.float32, jnp.bfloat16
    inverse = 1.0 / math.sqrt(HEAD_SIZE)

    order = [lax.rem(me + o, n) for o in range(n)]

    def each_peer(body):
        for p in order[1:]:
            body(p)

    cache_copy = pltpu.make_async_copy(cache_hbm, cache, store_sem.at[0])
    wq_copies = {}
    for c in range(chunks):
        for k in range(pieces):
            at = (pl.ds(k * piece, piece), pl.ds(c * chunk_cols, chunk_cols))
            wq_copies[c, k] = pltpu.make_async_copy(
                wq_hbm.at[at], wq.at[at], wq_sem.at[c, k]
            )
            wq_copies[c, k].start()
        if c == 0:
            cache_copy.start()
    wk_copy = pltpu.make_async_copy(wk_hbm, wk, wkv_sem.at[0])
    wv_copy = pltpu.make_async_copy(wv_hbm, wv, wkv_sem.at[1])
    down_copy = pltpu.make_async_copy(down_hbm, down, store_sem.at[1])
    up_copy = pltpu.make_async_copy(up_hbm, up, store_sem.at[2])
    wk_copy.start()
    wv_copy.start()
    down_copy.start()
    up_copy.start()

    def wo_copy(p):
        cols = pl.ds(pl.multiple_of(p * out_cols, out_cols), out_cols)
        return pltpu.make_async_copy(wo_hbm.at[:, cols], wo.at[p], wo_sem.at[p])

    def start_wo(o, carry):
        wo_copy(lax.rem(me + 1 + o, n)).start()
        return carry

    lax.fori_loop(0, n, start_wo, 0)

    barrier = pltpu.get_barrier_semaphore()
    each_peer(lambda p: pl.semaphore_signal(barrier, inc=1, device_id={"tp": p}, device_id_type=MESH))
    pl.semaphore_signal(barrier, inc=1, device_id={"inst": other}, device_id_type=MESH)

    for s in range(steps):
        hidden[pl.ds(s * reqs, reqs), :] = hidden_ref[s].astype(f32)
    block = hidden[...]
    factor = lax.rsqrt(jnp.mean(block * block, axis=-1, keepdims=True) + 1e-05)
    gain = gain_ref[...].astype(f32)
    for i in range(width // 128):
        cols = slice(i * 128, (i + 1) * 128)
        normed[:, cols] = (hidden[:, cols] * factor * gain[i : i + 1, :]).astype(bf16)

    own_lengths = [lengths_ref[inst * reqs + r] for r in range(reqs)]

    def by_request(index, numbers):
        chosen = jnp.full(index.shape, numbers[0], jnp.int32)
        for r in range(1, reqs):
            chosen = jnp.where(index == r, numbers[r], chosen)
        return chosen

    row = lax.broadcasted_iota(jnp.int32, (rows, HEAD_SIZE), 0)
    lane = lax.broadcasted_iota(jnp.int32, (rows, HEAD_SIZE), 1)
    half = HEAD_SIZE // 2
    place = (by_request(row & (reqs - 1), own_lengths) + row // reqs).astype(f32)
    freqs = jnp.exp((lane & (half - 1)).astype(f32) * (-2.0 * math.log(THETA) / HEAD_SIZE))
    angle = place * freqs
    cosine = jnp.cos(angle)
    sine = jnp.where(lane < half, -1.0, 1.0) * jnp.sin(angle)

    def rotated(tensor):
        return (tensor * cosine + pltpu.roll(tensor, half, 1) * sine).astype(bf16)


    def pair(src, dst, k):
        return pltpu.make_async_remote_copy(
            src_ref=src,
            dst_ref=dst,
            send_sem=pair_send.at[k],
            recv_sem=pair_recv.at[k],
            device_id={"inst": other},
            device_id_type=MESH,
        )

    moving = pair(moved_out, moved_in, 0)

    def query_copy(c, owner, p):
        return pltpu.make_async_remote_copy(
            src_ref=query_all.at[c, owner],
            dst_ref=query_all.at[c, owner],
            send_sem=query_send.at[c, p],
            recv_sem=query_recv.at[c, owner],
            device_id={"tp": p},
            device_id_type=MESH,
        )

    for c in range(chunks):
        total = jnp.zeros((rows, chunk_cols), f32)
        for k in range(pieces):
            wq_copies[c, k].wait()
            total += jnp.dot(
                normed[:, k * piece : (k + 1) * piece],
                wq[k * piece : (k + 1) * piece, c * chunk_cols : (c + 1) * chunk_cols],
                preferred_element_type=f32,
            )
        total = total.astype(bf16).astype(f32)
        for h in range(chunk_heads):
            query_all[c, me, h * rows : (h + 1) * rows, :] = rotated(
                total[:, h * HEAD_SIZE : (h + 1) * HEAD_SIZE]
            )
        if c == 0:
            pl.semaphore_wait(barrier, n)
        each_peer(lambda p: query_copy(c, me, p).start())
        if c == 0:
            cache_copy.wait()
            for j in range(2):
                moved_out[j] = cache[leaving_ref[inst, j]]
            moving.start()

    moving.wait_recv()
    first, second = leaving_ref[inst, 0], leaving_ref[inst, 1]
    for r in range(reqs):
        leaves = jnp.logical_or(first == r, second == r)
        fresh = moved_in[jnp.where(second == r, 1, 0)]
        now = jnp.where(leaves, fresh, cache[r])
        for k in range(n):
            keys[k, r * positions : (r + 1) * positions, :] = now[
                :, k * HEAD_SIZE : (k + 1) * HEAD_SIZE
            ]
            values[k, r * positions : (r + 1) * positions, :] = now[
                :, kv_width + k * HEAD_SIZE : kv_width + (k + 1) * HEAD_SIZE
            ]

    chunk_rows = chunk_heads * rows
    wide = (chunk_rows, reqs * positions)
    row = lax.broadcasted_iota(jnp.int32, wide, 0)
    column = lax.broadcasted_iota(jnp.int32, wide, 1)
    request = column // positions
    at = me * positions + (column & (positions - 1))
    valid = (request == (row & (reqs - 1))) & (at < by_request(request, own_lengths))
    stat_lane = lax.broadcasted_iota(jnp.int32, (chunk_rows, 128), 1)

    def attend(query, key, value, mask):
        score = lax.dot_general(
            query, key, (((1,), (1,)), ((), ())), preferred_element_type=f32
        )
        score = jnp.where(mask, score * inverse, NEGATIVE)
        top = jnp.max(score, axis=-1, keepdims=True)
        weight = jnp.where(mask, jnp.exp(score - top), 0.0)
        total = jnp.sum(weight, axis=-1, keepdims=True)
        mixed = jnp.dot(weight.astype(bf16), value, preferred_element_type=f32)
        total = jnp.where(total > 0.0, total, 1.0)
        return mixed / total, top + jnp.log(total)

    def part_copy(c, owner, p):
        return pltpu.make_async_remote_copy(
            src_ref=part_out.at[c, p],
            dst_ref=part_in.at[c, owner],
            send_sem=part_send.at[c, p],
            recv_sem=part_recv.at[c, owner],
            device_id={"tp": p},
            device_id_type=MESH,
        )

    extra = lax.broadcasted_iota(jnp.int32, (16, 128), 0)

    def attend_some(c, some):
        for o in some:
            if o > 0:
                query_copy(c, order[o], order[o]).wait_recv()
        parts = [attend(query_all[c, order[o]], keys[order[o]], values[order[o]], valid) for o in some]
        levels = jnp.zeros((chunk_rows, 128), f32)
        for o, (_, level) in zip(some, parts):
            levels = jnp.where(stat_lane == o, level, levels)
        if chunk_rows < 128:
            levels = jnp.concatenate([levels, jnp.zeros((128 - chunk_rows, 128), f32)], axis=0)
        levels = jnp.transpose(levels)
        for o, (mixed, _) in zip(some, parts):
            level = levels[o : o + 1, :]
            high = level.astype(bf16).astype(f32)
            middle = (level - high).astype(bf16).astype(f32)
            low = level - high - middle
            split = jnp.where(extra == 0, high, jnp.where(extra == 1, middle, jnp.where(extra == 2, low, 0.0)))
            target = part_in.at[c, me] if o == 0 else part_out.at[c, order[o]]
            target[:chunk_rows, :] = mixed.astype(bf16)
            target[chunk_rows:, :] = split.astype(bf16)
            if o > 0:
                part_copy(c, me, order[o]).start()

    def attend_chunk(c):
        for begin in range(0, n, GROUP):
            attend_some(c, range(begin, begin + GROUP))

    attend_chunk(0)

    def page_of(index):
        page = table_ref[adapter_ref[index]]
        return jnp.clip(page - inst * store, 0, store - 1), page // store == inst

    down_copy.wait()
    up_copy.wait()
    for r in range(reqs):
        local, _ = page_of(other * reqs + r)
        down_out[r] = down[local]
        up_out[r] = up[local]
    down_pair = pair(down_out, down_in, 1)
    up_pair = pair(up_out, up_in, 2)
    down_pair.start()
    up_pair.start()

    for c in range(1, chunks):
        attend_chunk(c)

    wk_copy.wait()
    key_new = jnp.dot(normed[...], wk[...], preferred_element_type=f32).astype(bf16)
    key_new = rotated(key_new.astype(f32))
    wv_copy.wait()
    value_new = jnp.dot(normed[...], wv[...], preferred_element_type=f32).astype(bf16)

    small = (chunk_rows, rows)
    row = lax.broadcasted_iota(jnp.int32, small, 0)
    column = lax.broadcasted_iota(jnp.int32, small, 1)
    causal = ((row & (reqs - 1)) == (column & (reqs - 1))) & (
        column // reqs <= (row & (rows - 1)) // reqs
    )
    fresh_parts = [attend(query_all[c, me], key_new, value_new, causal) for c in range(chunks)]

    down_pair.wait_recv()
    up_pair.wait_recv()
    for r in range(reqs):
        local, held = page_of(inst * reqs + r)
        down_in[r] = jnp.where(held, down[local], down_in[r])
        up_in[r] = jnp.where(held, up[local], up_in[r])

    for c in range(chunks):
        each_peer(lambda p: part_copy(c, p, p).wait_recv())
    sub = lax.broadcasted_iota(jnp.int32, (8, 128), 0)
    heads = []
    for c in range(chunks):
        fresh_mixed, fresh_level = fresh_parts[c]
        level = jnp.zeros((8, 128), f32)
        for p in range(n):
            split = jnp.sum(part_in[c, p, chunk_rows:, :].astype(f32), axis=0, keepdims=True)
            level = jnp.where(sub == p, split, level)
        level = jnp.transpose(level)[:chunk_rows, :]
        top = jnp.maximum(jnp.max(level, axis=-1, keepdims=True), fresh_level)
        weight = jnp.exp(level - top)
        fresh_weight = jnp.exp(fresh_level - top)
        total = jnp.sum(weight, axis=-1, keepdims=True) + fresh_weight
        mixed = fresh_mixed * fresh_weight
        for p in range(n):
            mixed += part_in[c, p, :chunk_rows, :].astype(f32) * weight[:, p : p + 1]
        mixed = (mixed / total).astype(bf16)
        heads += [mixed[h * rows : (h + 1) * rows, :] for h in range(chunk_heads)]
    attended = jnp.concatenate(heads, axis=1)

    def shrink_copy(owner, p):
        return pltpu.make_async_remote_copy(
            src_ref=shrink_part,
            dst_ref=shrink_in.at[owner],
            send_sem=shrink_send.at[p],
            recv_sem=shrink_recv.at[owner],
            device_id={"tp": p},
            device_id_type=MESH,
        )

    row = lax.broadcasted_iota(jnp.int32, (rows, rank), 0) & (reqs - 1)
    shrunk = jnp.zeros((rows, rank), f32)
    for r in range(reqs):
        product = lax.dot_general(
            attended, down_in[r], (((1,), (1,)), ((), ())), preferred_element_type=f32
        )
        shrunk = jnp.where(row == r, product, shrunk)
    shrink_part[...] = shrunk
    each_peer(lambda p: shrink_copy(me, p).start())

    def base_copy(owner, p):
        return pltpu.make_async_remote_copy(
            src_ref=base_out.at[p],
            dst_ref=base_in.at[owner],
            send_sem=base_send.at[p],
            recv_sem=base_recv.at[owner],
            device_id={"tp": p},
            device_id_type=MESH,
        )

    def peer_block(p):
        wo_copy(p).wait()
        base_out[p] = jnp.dot(attended, wo[p], preferred_element_type=f32).astype(bf16)
        base_copy(me, p).start()

    each_peer(peer_block)
    wo_copy(me).wait()
    output = jnp.dot(attended, wo[me], preferred_element_type=f32)

    each_peer(lambda p: shrink_copy(p, p).wait_recv())
    shrink_in[me] = shrink_part[...]
    shrunk = shrink_in[0]
    for p in range(1, n):
        shrunk += shrink_in[p]
    shrunk = shrunk.astype(bf16)
    delta = jnp.zeros((rows, out_cols), f32)
    for r in range(reqs):
        chosen = jnp.where(row == r, shrunk.astype(f32), 0.0).astype(bf16)
        delta += jnp.dot(chosen, up_in[r], preferred_element_type=f32)
    output += ADAPTER_SCALE * delta
    moving.wait_send()
    down_pair.wait_send()
    up_pair.wait_send()

    def sent(p):
        for c in range(chunks):
            query_copy(c, me, p).wait_send()
            part_copy(c, me, p).wait_send()
        shrink_copy(me, p).wait_send()

    each_peer(sent)

    each_peer(lambda p: base_copy(p, p).wait_recv())
    base_in[me] = jnp.zeros((rows, out_cols), bf16)
    for p in range(n):
        output += base_in[p].astype(f32)
    hidden[:, :out_cols] = output
    for s in range(steps):
        out_ref[s] = hidden[pl.ds(s * reqs, reqs), :out_cols].astype(bf16)

    each_peer(lambda p: base_copy(me, p).wait_send())


CHUNKS = 2
GROUP = 8
PIECES = 4


def fused(
    hidden_input,
    input_norm_gain,
    query_weight,
    key_weight,
    value_weight,
    output_weight,
    key_value_cache,
    lengths,
    leaving,
    request_adapter_index,
    adapter_page_table,
    adapter_down_pages,
    adapter_up_pages,
):
    n = lax.axis_size("tp")
    steps, reqs, width = hidden_input.shape
    head_cols = query_weight.shape[1]
    positions, kv_both = key_value_cache.shape[1:]
    store, _, rank = adapter_down_pages.shape
    out_cols = adapter_up_pages.shape[2]
    rows = steps * reqs
    chunk_rows = head_cols // HEAD_SIZE // CHUNKS * rows
    dims = (n, steps, reqs, width, head_cols, positions, store, rank, out_cols, CHUNKS, PIECES)
    bf16, f32 = jnp.bfloat16, jnp.float32
    dma = pltpu.SemaphoreType.DMA
    vmem = pl.BlockSpec(memory_space=pltpu.VMEM)
    smem = pl.BlockSpec(memory_space=pltpu.SMEM)
    hbm = pl.BlockSpec(memory_space=pl.ANY)
    return pl.pallas_call(
        functools.partial(fused_kernel, dims),
        out_shape=jax.ShapeDtypeStruct((steps, reqs, out_cols), bf16),
        in_specs=[vmem, vmem, hbm, hbm, hbm, hbm, hbm, smem, smem, smem, smem, hbm, hbm],
        out_specs=vmem,
        scratch_shapes=[
            pltpu.VMEM((width, head_cols), bf16),
            pltpu.VMEM((width, HEAD_SIZE), bf16),
            pltpu.VMEM((width, HEAD_SIZE), bf16),
            pltpu.VMEM((n, head_cols, out_cols), bf16),
            pltpu.VMEM((reqs, positions, kv_both), bf16),
            pltpu.VMEM((2, positions, kv_both), bf16),
            pltpu.VMEM((2, positions, kv_both), bf16),
            pltpu.VMEM((n, reqs * positions, HEAD_SIZE), bf16),
            pltpu.VMEM((n, reqs * positions, HEAD_SIZE), bf16),
            pltpu.VMEM((store, rank, head_cols), bf16),
            pltpu.VMEM((store, rank, out_cols), bf16),
            pltpu.VMEM((reqs, rank, head_cols), bf16),
            pltpu.VMEM((reqs, rank, out_cols), bf16),
            pltpu.VMEM((reqs, rank, head_cols), bf16),
            pltpu.VMEM((reqs, rank, out_cols), bf16),
            pltpu.VMEM((rows, width), f32),
            pltpu.VMEM((rows, width), bf16),
            pltpu.VMEM((CHUNKS, n, chunk_rows, HEAD_SIZE), bf16),
            pltpu.VMEM((CHUNKS, n, chunk_rows + 16, HEAD_SIZE), bf16),
            pltpu.VMEM((CHUNKS, n, chunk_rows + 16, HEAD_SIZE), bf16),
            pltpu.VMEM((rows, rank), f32),
            pltpu.VMEM((n, rows, rank), f32),
            pltpu.VMEM((n, rows, out_cols), bf16),
            pltpu.VMEM((n, rows, out_cols), bf16),
            dma((CHUNKS, PIECES)),
            dma((2,)),
            dma((n,)),
            dma((3,)),
            dma((3,)),
            dma((3,)),
            dma((CHUNKS, n)),
            dma((CHUNKS, n)),
            dma((CHUNKS, n)),
            dma((CHUNKS, n)),
            dma((n,)),
            dma((n,)),
            dma((n,)),
            dma((n,)),
        ],
        compiler_params=pltpu.CompilerParams(
            collective_id=0, has_side_effects=True, vmem_limit_bytes=60 * 1024 * 1024
        ),
        name="fused",
    )(
        hidden_input,
        input_norm_gain.reshape(width // 128, 128),
        query_weight,
        key_weight,
        value_weight,
        output_weight,
        key_value_cache,
        lengths,
        leaving,
        request_adapter_index,
        adapter_page_table,
        jnp.swapaxes(adapter_down_pages, 1, 2),
        adapter_up_pages,
    )


def solution(mesh):
    body = fused if mesh.shape["tp"] == KVH and mesh.shape["inst"] == 2 else shards
    return jax.shard_map(
        body,
        mesh=mesh,
        in_specs=(
            P(None, ("groups", "inst"), None),
            P(),
            P(None, "tp"),
            P(None, "tp"),
            P(None, "tp"),
            P("tp", None),
            P(("groups", "inst"), "tp", None),
            P("groups"),
            P("groups", None),
            P("groups"),
            P(),
            P("inst", "tp", None),
            P("inst", None, "tp"),
        ),
        out_specs=P(None, ("groups", "inst"), "tp"),
        check_vma=False,
    )
```

```python
import functools
import math

import jax
import jax.numpy as jnp
from jax import lax
from jax.experimental import pallas as pl
from jax.experimental.pallas import tpu as pltpu
from jax.sharding import PartitionSpec as P

QUERY_HEADS = 64
KVH = 8
HEAD_SIZE = 128
MESH = pl.DeviceIdType.MESH


THETA = 500000.0
ADAPTER_SCALE = 0.5
NEGATIVE = -1e30


def partner(block, axis, bit):
    count = lax.axis_size(axis)
    route = []
    for low in range(count):
        high = low | 1 << bit
        if high != low and high < count:
            route += [(low, high), (high, low)]
    return lax.ppermute(block, axis, route)


def combined_all(value, axis, combine):
    everything = jax.tree.map(
        lambda part, kind: lax.all_gather(part.astype(kind), axis),
        value,
        (jnp.bfloat16, jnp.bfloat16, jnp.bfloat16),
    )

    def take(k):
        return jax.tree.map(lambda part, own: part[k].astype(own.dtype), everything, value)

    return lax.fori_loop(
        1, lax.axis_size(axis), lambda k, so_far: combine(so_far, take(k)), take(0)
    )


def normalize(hidden, input_norm_gain):
    values = hidden.astype(jnp.float32)
    factor = lax.rsqrt(jnp.mean(values * values, axis=-1, keepdims=True) + 1e-05)
    return (values * factor * input_norm_gain.astype(jnp.float32)).astype(jnp.bfloat16)


def rotate(tensor, position):
    middle = tensor.shape[-1] // 2
    freqs = jnp.exp(
        jnp.arange(middle, dtype=jnp.float32) * (-2.0 * math.log(THETA) / tensor.shape[-1])
    )
    angles = position[..., None] * freqs
    cosine = jnp.cos(angles)
    sine_part = jnp.sin(angles)
    first = tensor[..., :middle]
    second = tensor[..., middle:]
    return jnp.concatenate(
        [first * cosine - second * sine_part, second * cosine + first * sine_part], axis=-1
    )


def combine(earlier, later):
    top_first, total_first, mixed_first = earlier
    top_second, total_second, mixed_second = later
    top = jnp.maximum(top_first, top_second)
    scale_first = jnp.exp(top_first - top)
    scale_second = jnp.exp(top_second - top)
    total = total_first * scale_first + total_second * scale_second
    mixed = mixed_first * scale_first[..., None] + mixed_second * scale_second[..., None]
    return (top, total, mixed)


def shards(
    hidden_input,
    input_norm_gain,
    query_weight,
    key_weight,
    value_weight,
    output_weight,
    key_value_cache,
    lengths,
    leaving,
    request_adapter_index,
    adapter_page_table,
    adapter_down_pages,
    adapter_up_pages,
):
    decode_steps, request_rows, width = hidden_input.shape
    device = lax.axis_index("tp")
    instance = lax.axis_index("inst")
    head_cols = query_weight.shape[1]
    local_heads = head_cols // HEAD_SIZE
    positions = key_value_cache.shape[1]
    kv_width = KVH * HEAD_SIZE
    group = QUERY_HEADS // KVH
    normed = normalize(hidden_input, input_norm_gain).reshape(decode_steps * request_rows, width)
    query_part = jnp.dot(normed, query_weight, preferred_element_type=jnp.float32).astype(
        jnp.bfloat16
    )
    key_part = jnp.dot(normed, key_weight, preferred_element_type=jnp.float32).astype(jnp.bfloat16)
    value_part = jnp.dot(normed, value_weight, preferred_element_type=jnp.float32).astype(
        jnp.bfloat16
    )
    query_all, key_all, value_all = (
        lax.all_gather(query_part, "tp", axis=1, tiled=True),
        lax.all_gather(key_part, "tp", axis=1, tiled=True),
        lax.all_gather(value_part, "tp", axis=1, tiled=True),
    )
    lengths_here = lax.dynamic_slice_in_dim(lengths, instance * request_rows, request_rows)
    new_pos = (lengths_here[None, :] + jnp.arange(decode_steps, dtype=jnp.int32)[:, None]).astype(
        jnp.float32
    )[:, :, None]
    query_rot = rotate(
        query_all.reshape(decode_steps, request_rows, QUERY_HEADS, HEAD_SIZE).astype(jnp.float32),
        new_pos,
    ).astype(jnp.bfloat16)
    query_rot = query_rot.reshape(decode_steps, request_rows, KVH, group, HEAD_SIZE)
    key_rot = rotate(
        key_all.reshape(decode_steps, request_rows, KVH, HEAD_SIZE).astype(jnp.float32), new_pos
    ).astype(jnp.bfloat16)
    value_new = value_all.reshape(decode_steps, request_rows, KVH, HEAD_SIZE)
    outgoing_slots = lax.dynamic_index_in_dim(leaving, instance, 0, keepdims=False)
    arriving = partner(key_value_cache[outgoing_slots], "inst", 0)
    cache_now = key_value_cache.at[outgoing_slots].set(arriving)
    pages = adapter_page_table[request_adapter_index]
    adapter_store_size = adapter_down_pages.shape[0]
    own_pages = lax.dynamic_slice_in_dim(pages, instance * request_rows, request_rows)
    partner_pages = lax.dynamic_slice_in_dim(pages, (1 - instance) * request_rows, request_rows)

    def select_pages(wanted):
        local_page_index = jnp.clip(
            wanted - instance * adapter_store_size, 0, adapter_store_size - 1
        )
        down_matrix_flat = adapter_down_pages[local_page_index].reshape(request_rows, -1)
        up_matrix_flat = adapter_up_pages[local_page_index].reshape(request_rows, -1)
        return (
            jnp.concatenate([down_matrix_flat, up_matrix_flat], axis=1),
            wanted // adapter_store_size == instance,
        )

    outgoing_pages, held_there = select_pages(partner_pages)
    outgoing_pages = jnp.where(held_there[:, None], outgoing_pages, jnp.zeros_like(outgoing_pages))
    arriving_pages = partner(outgoing_pages, "inst", 0)
    local_pages, held_here = select_pages(own_pages)
    fetched_pages = jnp.where(held_here[:, None], local_pages, arriving_pages)
    down_matrix_size = adapter_down_pages.shape[1] * adapter_down_pages.shape[2]
    down_matrix_rows = fetched_pages[:, :down_matrix_size].reshape(
        request_rows, adapter_down_pages.shape[1], adapter_down_pages.shape[2]
    )
    up_matrix_rows = fetched_pages[:, down_matrix_size:].reshape(
        request_rows, adapter_up_pages.shape[1], adapter_up_pages.shape[2]
    )
    keys = cache_now[:, :, :kv_width].reshape(request_rows, positions, KVH, HEAD_SIZE)
    values = cache_now[:, :, kv_width:].reshape(request_rows, positions, KVH, HEAD_SIZE)
    place = device * positions + jnp.arange(positions, dtype=jnp.int32)
    valid = place[None, :] < lengths_here[:, None]
    valid_b = valid[None, :, None, None, :]
    inverse = 1.0 / math.sqrt(HEAD_SIZE)
    cache_scores = (
        jnp.einsum("srkgd,rpkd->srkgp", query_rot, keys, preferred_element_type=jnp.float32)
        * inverse
    )
    cache_scores = jnp.where(valid_b, cache_scores, NEGATIVE)
    new_scores = (
        jnp.einsum("srkgd,trkd->srkgt", query_rot, key_rot, preferred_element_type=jnp.float32)
        * inverse
    )
    causal = (jnp.arange(decode_steps)[None, :] <= jnp.arange(decode_steps)[:, None]) & (
        device == 0
    )
    causal_b = causal[:, None, None, None, :]
    new_scores = jnp.where(causal_b, new_scores, NEGATIVE)
    top = jnp.maximum(cache_scores.max(-1), new_scores.max(-1))
    cache_weights = jnp.exp(cache_scores - top[..., None]) * valid_b.astype(jnp.float32)
    new_weights = jnp.exp(new_scores - top[..., None]) * causal_b.astype(jnp.float32)
    total = cache_weights.sum(-1) + new_weights.sum(-1)
    mixed = jnp.einsum(
        "srkgp,rpkd->srkgd",
        cache_weights.astype(jnp.bfloat16),
        values,
        preferred_element_type=jnp.float32,
    )
    mixed = mixed + jnp.einsum(
        "srkgt,trkd->srkgd",
        new_weights.astype(jnp.bfloat16),
        value_new,
        preferred_element_type=jnp.float32,
    )
    top = top.reshape(decode_steps, request_rows, QUERY_HEADS)
    total = total.reshape(decode_steps, request_rows, QUERY_HEADS)
    mixed = mixed.reshape(decode_steps, request_rows, QUERY_HEADS, HEAD_SIZE)
    top_all, total_all, mixed_all = combined_all((top, total, mixed), "tp", combine)
    first_head = device * local_heads
    total_own = lax.dynamic_slice_in_dim(total_all, first_head, local_heads, 2)
    mixed_own = lax.dynamic_slice_in_dim(mixed_all, first_head, local_heads, 2)
    attention_output = mixed_own / total_own[..., None]
    attention_output = attention_output.astype(jnp.bfloat16).reshape(
        decode_steps * request_rows, head_cols
    )
    base_part = jnp.dot(attention_output, output_weight, preferred_element_type=jnp.float32)
    shrink_part = jnp.einsum(
        "src,rck->srk",
        attention_output.reshape(decode_steps, request_rows, head_cols),
        down_matrix_rows,
        preferred_element_type=jnp.float32,
    )
    shrunk_output = lax.psum(shrink_part, "tp")
    base_output = lax.psum_scatter(
        base_part.astype(jnp.bfloat16), "tp", scatter_dimension=1, tiled=True
    ).astype(jnp.float32)
    shrunk_output = shrunk_output.astype(jnp.bfloat16)
    adapter_delta = jnp.einsum(
        "srk,rkd->srd", shrunk_output, up_matrix_rows, preferred_element_type=jnp.float32
    )
    return (
        base_output.reshape(decode_steps, request_rows, -1) + ADAPTER_SCALE * adapter_delta
    ).astype(jnp.bfloat16)


def fused_kernel(
    dims,
    hidden_ref,
    gain_ref,
    wq_hbm,
    wk_hbm,
    wv_hbm,
    wo_hbm,
    cache_hbm,
    lengths_ref,
    leaving_ref,
    adapter_ref,
    table_ref,
    down_hbm,
    up_hbm,
    out_ref,
    wq,
    wk,
    wv,
    wo,
    cache,
    moved_out,
    moved_in,
    keys,
    values,
    down,
    up,
    down_out,
    up_out,
    down_in,
    up_in,
    hidden,
    normed,
    query_all,
    part_out,
    part_in,
    shrink_part,
    shrink_in,
    base_out,
    base_in,
    wq_sem,
    wkv_sem,
    wo_sem,
    store_sem,
    pair_send,
    pair_recv,
    query_send,
    query_recv,
    part_send,
    part_recv,
    shrink_send,
    shrink_recv,
    base_send,
    base_recv,
):
    n, steps, reqs, width, head_cols, positions, store, rank, out_cols, chunks, pieces = dims
    rows = steps * reqs
    head_count = head_cols // HEAD_SIZE
    chunk_heads = head_count // chunks
    chunk_cols = chunk_heads * HEAD_SIZE
    piece = width // pieces
    kv_width = n * HEAD_SIZE
    me = lax.axis_index("tp")
    inst = lax.axis_index("inst")
    other = 1 - inst
    f32, bf16 = jnp.float32, jnp.bfloat16
    inverse = 1.0 / math.sqrt(HEAD_SIZE)

    order = [lax.rem(me + o, n) for o in range(n)]

    def each_peer(body):
        for p in order[1:]:
            body(p)

    cache_copy = pltpu.make_async_copy(cache_hbm, cache, store_sem.at[0])
    wq_copies = {}
    for c in range(chunks):
        for k in range(pieces):
            at = (pl.ds(k * piece, piece), pl.ds(c * chunk_cols, chunk_cols))
            wq_copies[c, k] = pltpu.make_async_copy(
                wq_hbm.at[at], wq.at[at], wq_sem.at[c, k]
            )
            wq_copies[c, k].start()
        if c == 0:
            cache_copy.start()
    wk_copy = pltpu.make_async_copy(wk_hbm, wk, wkv_sem.at[0])
    wv_copy = pltpu.make_async_copy(wv_hbm, wv, wkv_sem.at[1])
    down_copy = pltpu.make_async_copy(down_hbm, down, store_sem.at[1])
    up_copy = pltpu.make_async_copy(up_hbm, up, store_sem.at[2])

    def wo_copy(p):
        cols = pl.ds(pl.multiple_of(p * out_cols, out_cols), out_cols)
        return pltpu.make_async_copy(wo_hbm.at[:, cols], wo.at[p], wo_sem.at[p])

    def start_wo(o, carry):
        wo_copy(lax.rem(me + 1 + o, n)).start()
        return carry


    barrier = pltpu.get_barrier_semaphore()
    each_peer(lambda p: pl.semaphore_signal(barrier, inc=1, device_id={"tp": p}, device_id_type=MESH))
    pl.semaphore_signal(barrier, inc=1, device_id={"inst": other}, device_id_type=MESH)

    for s in range(steps):
        hidden[pl.ds(s * reqs, reqs), :] = hidden_ref[s].astype(f32)
    block = hidden[...]
    factor = lax.rsqrt(jnp.mean(block * block, axis=-1, keepdims=True) + 1e-05)
    gain = gain_ref[...].astype(f32)
    for i in range(width // 128):
        cols = slice(i * 128, (i + 1) * 128)
        normed[:, cols] = (hidden[:, cols] * factor * gain[i : i + 1, :]).astype(bf16)

    own_lengths = [lengths_ref[inst * reqs + r] for r in range(reqs)]

    def by_request(index, numbers):
        chosen = jnp.full(index.shape, numbers[0], jnp.int32)
        for r in range(1, reqs):
            chosen = jnp.where(index == r, numbers[r], chosen)
        return chosen

    row = lax.broadcasted_iota(jnp.int32, (rows, HEAD_SIZE), 0)
    lane = lax.broadcasted_iota(jnp.int32, (rows, HEAD_SIZE), 1)
    half = HEAD_SIZE // 2
    place = (by_request(row & (reqs - 1), own_lengths) + row // reqs).astype(f32)
    freqs = jnp.exp((lane & (half - 1)).astype(f32) * (-2.0 * math.log(THETA) / HEAD_SIZE))
    angle = place * freqs
    cosine = jnp.cos(angle)
    sine = jnp.where(lane < half, -1.0, 1.0) * jnp.sin(angle)

    def rotated(tensor):
        return (tensor * cosine + pltpu.roll(tensor, half, 1) * sine).astype(bf16)


    def pair(src, dst, k):
        return pltpu.make_async_remote_copy(
            src_ref=src,
            dst_ref=dst,
            send_sem=pair_send.at[k],
            recv_sem=pair_recv.at[k],
            device_id={"inst": other},
            device_id_type=MESH,
        )

    moving = pair(moved_out, moved_in, 0)

    def query_copy(c, owner, p):
        return pltpu.make_async_remote_copy(
            src_ref=query_all.at[c, owner],
            dst_ref=query_all.at[c, owner],
            send_sem=query_send.at[c, p],
            recv_sem=query_recv.at[c, owner],
            device_id={"tp": p},
            device_id_type=MESH,
        )

    for c in range(chunks):
        total = jnp.zeros((rows, chunk_cols), f32)
        for k in range(pieces):
            wq_copies[c, k].wait()
            total += jnp.dot(
                normed[:, k * piece : (k + 1) * piece],
                wq[k * piece : (k + 1) * piece, c * chunk_cols : (c + 1) * chunk_cols],
                preferred_element_type=f32,
            )
        total = total.astype(bf16).astype(f32)
        for h in range(chunk_heads):
            query_all[c, me, h * rows : (h + 1) * rows, :] = rotated(
                total[:, h * HEAD_SIZE : (h + 1) * HEAD_SIZE]
            )
        if c == 0:
            pl.semaphore_wait(barrier, n)
        each_peer(lambda p: query_copy(c, me, p).start())
        if c == 0:
            cache_copy.wait()
            for j in range(2):
                moved_out[j] = cache[leaving_ref[inst, j]]
            moving.start()

    wk_copy.start()
    wv_copy.start()
    down_copy.start()
    up_copy.start()
    moving.wait_recv()
    first, second = leaving_ref[inst, 0], leaving_ref[inst, 1]
    for r in range(reqs):
        leaves = jnp.logical_or(first == r, second == r)
        fresh = moved_in[jnp.where(second == r, 1, 0)]
        now = jnp.where(leaves, fresh, cache[r])
        for k in range(n):
            keys[k, r * positions : (r + 1) * positions, :] = now[
                :, k * HEAD_SIZE : (k + 1) * HEAD_SIZE
            ]
            values[k, r * positions : (r + 1) * positions, :] = now[
                :, kv_width + k * HEAD_SIZE : kv_width + (k + 1) * HEAD_SIZE
            ]

    chunk_rows = chunk_heads * rows
    wide = (chunk_rows, reqs * positions)
    row = lax.broadcasted_iota(jnp.int32, wide, 0)
    column = lax.broadcasted_iota(jnp.int32, wide, 1)
    request = column // positions
    at = me * positions + (column & (positions - 1))
    valid = (request == (row & (reqs - 1))) & (at < by_request(request, own_lengths))
    stat_lane = lax.broadcasted_iota(jnp.int32, (chunk_rows, 128), 1)

    def attend(query, key, value, mask):
        score = lax.dot_general(
            query, key, (((1,), (1,)), ((), ())), preferred_element_type=f32
        )
        score = jnp.where(mask, score * inverse, NEGATIVE)
        top = jnp.max(score, axis=-1, keepdims=True)
        weight = jnp.where(mask, jnp.exp(score - top), 0.0)
        total = jnp.sum(weight, axis=-1, keepdims=True)
        mixed = jnp.dot(weight.astype(bf16), value, preferred_element_type=f32)
        total = jnp.where(total > 0.0, total, 1.0)
        return mixed / total, top + jnp.log(total)

    def part_copy(c, owner, p):
        return pltpu.make_async_remote_copy(
            src_ref=part_out.at[c, p],
            dst_ref=part_in.at[c, owner],
            send_sem=part_send.at[c, p],
            recv_sem=part_recv.at[c, owner],
            device_id={"tp": p},
            device_id_type=MESH,
        )

    extra = lax.broadcasted_iota(jnp.int32, (16, 128), 0)

    def attend_some(c, some):
        for o in some:
            if o > 0:
                query_copy(c, order[o], order[o]).wait_recv()
        parts = [attend(query_all[c, order[o]], keys[order[o]], values[order[o]], valid) for o in some]
        levels = jnp.zeros((chunk_rows, 128), f32)
        for o, (_, level) in zip(some, parts):
            levels = jnp.where(stat_lane == o, level, levels)
        if chunk_rows < 128:
            levels = jnp.concatenate([levels, jnp.zeros((128 - chunk_rows, 128), f32)], axis=0)
        levels = jnp.transpose(levels)
        for o, (mixed, _) in zip(some, parts):
            level = levels[o : o + 1, :]
            high = level.astype(bf16).astype(f32)
            middle = (level - high).astype(bf16).astype(f32)
            low = level - high - middle
            split = jnp.where(extra == 0, high, jnp.where(extra == 1, middle, jnp.where(extra == 2, low, 0.0)))
            target = part_in.at[c, me] if o == 0 else part_out.at[c, order[o]]
            target[:chunk_rows, :] = mixed.astype(bf16)
            target[chunk_rows:, :] = split.astype(bf16)
            if o > 0:
                part_copy(c, me, order[o]).start()

    def attend_chunk(c):
        for begin in range(0, n, GROUP):
            attend_some(c, range(begin, begin + GROUP))

    attend_chunk(0)

    def page_of(index):
        page = table_ref[adapter_ref[index]]
        return jnp.clip(page - inst * store, 0, store - 1), page // store == inst

    down_copy.wait()
    up_copy.wait()
    for r in range(reqs):
        local, _ = page_of(other * reqs + r)
        down_out[r] = down[local]
        up_out[r] = up[local]
    down_pair = pair(down_out, down_in, 1)
    up_pair = pair(up_out, up_in, 2)
    down_pair.start()
    up_pair.start()

    for c in range(1, chunks):
        attend_chunk(c)

    lax.fori_loop(0, n, start_wo, 0)
    wk_copy.wait()
    key_new = jnp.dot(normed[...], wk[...], preferred_element_type=f32).astype(bf16)
    key_new = rotated(key_new.astype(f32))
    wv_copy.wait()
    value_new = jnp.dot(normed[...], wv[...], preferred_element_type=f32).astype(bf16)

    small = (chunk_rows, rows)
    row = lax.broadcasted_iota(jnp.int32, small, 0)
    column = lax.broadcasted_iota(jnp.int32, small, 1)
    causal = ((row & (reqs - 1)) == (column & (reqs - 1))) & (
        column // reqs <= (row & (rows - 1)) // reqs
    )
    fresh_parts = [attend(query_all[c, me], key_new, value_new, causal) for c in range(chunks)]

    down_pair.wait_recv()
    up_pair.wait_recv()
    for r in range(reqs):
        local, held = page_of(inst * reqs + r)
        down_in[r] = jnp.where(held, down[local], down_in[r])
        up_in[r] = jnp.where(held, up[local], up_in[r])

    for c in range(chunks):
        each_peer(lambda p: part_copy(c, p, p).wait_recv())
    sub = lax.broadcasted_iota(jnp.int32, (8, 128), 0)
    heads = []
    for c in range(chunks):
        fresh_mixed, fresh_level = fresh_parts[c]
        level = jnp.zeros((8, 128), f32)
        for p in range(n):
            split = jnp.sum(part_in[c, p, chunk_rows:, :].astype(f32), axis=0, keepdims=True)
            level = jnp.where(sub == p, split, level)
        level = jnp.transpose(level)[:chunk_rows, :]
        top = jnp.maximum(jnp.max(level, axis=-1, keepdims=True), fresh_level)
        weight = jnp.exp(level - top)
        fresh_weight = jnp.exp(fresh_level - top)
        total = jnp.sum(weight, axis=-1, keepdims=True) + fresh_weight
        mixed = fresh_mixed * fresh_weight
        for p in range(n):
            mixed += part_in[c, p, :chunk_rows, :].astype(f32) * weight[:, p : p + 1]
        mixed = (mixed / total).astype(bf16)
        heads += [mixed[h * rows : (h + 1) * rows, :] for h in range(chunk_heads)]
    attended = jnp.concatenate(heads, axis=1)

    def shrink_copy(owner, p):
        return pltpu.make_async_remote_copy(
            src_ref=shrink_part,
            dst_ref=shrink_in.at[owner],
            send_sem=shrink_send.at[p],
            recv_sem=shrink_recv.at[owner],
            device_id={"tp": p},
            device_id_type=MESH,
        )

    row = lax.broadcasted_iota(jnp.int32, (rows, rank), 0) & (reqs - 1)
    shrunk = jnp.zeros((rows, rank), f32)
    for r in range(reqs):
        product = lax.dot_general(
            attended, down_in[r], (((1,), (1,)), ((), ())), preferred_element_type=f32
        )
        shrunk = jnp.where(row == r, product, shrunk)
    shrink_part[...] = shrunk
    each_peer(lambda p: shrink_copy(me, p).start())

    def base_copy(owner, p):
        return pltpu.make_async_remote_copy(
            src_ref=base_out.at[p],
            dst_ref=base_in.at[owner],
            send_sem=base_send.at[p],
            recv_sem=base_recv.at[owner],
            device_id={"tp": p},
            device_id_type=MESH,
        )

    def peer_block(p):
        wo_copy(p).wait()
        base_out[p] = jnp.dot(attended, wo[p], preferred_element_type=f32).astype(bf16)
        base_copy(me, p).start()

    each_peer(peer_block)
    wo_copy(me).wait()
    output = jnp.dot(attended, wo[me], preferred_element_type=f32)

    each_peer(lambda p: shrink_copy(p, p).wait_recv())
    shrink_in[me] = shrink_part[...]
    shrunk = shrink_in[0]
    for p in range(1, n):
        shrunk += shrink_in[p]
    shrunk = shrunk.astype(bf16)
    delta = jnp.zeros((rows, out_cols), f32)
    for r in range(reqs):
        chosen = jnp.where(row == r, shrunk.astype(f32), 0.0).astype(bf16)
        delta += jnp.dot(chosen, up_in[r], preferred_element_type=f32)
    output += ADAPTER_SCALE * delta
    moving.wait_send()
    down_pair.wait_send()
    up_pair.wait_send()

    def sent(p):
        for c in range(chunks):
            query_copy(c, me, p).wait_send()
            part_copy(c, me, p).wait_send()
        shrink_copy(me, p).wait_send()

    each_peer(sent)

    each_peer(lambda p: base_copy(p, p).wait_recv())
    base_in[me] = jnp.zeros((rows, out_cols), bf16)
    for p in range(n):
        output += base_in[p].astype(f32)
    hidden[:, :out_cols] = output
    for s in range(steps):
        out_ref[s] = hidden[pl.ds(s * reqs, reqs), :out_cols].astype(bf16)

    each_peer(lambda p: base_copy(me, p).wait_send())


CHUNKS = 2
GROUP = 8
PIECES = 4


def fused(
    hidden_input,
    input_norm_gain,
    query_weight,
    key_weight,
    value_weight,
    output_weight,
    key_value_cache,
    lengths,
    leaving,
    request_adapter_index,
    adapter_page_table,
    adapter_down_pages,
    adapter_up_pages,
):
    n = lax.axis_size("tp")
    steps, reqs, width = hidden_input.shape
    head_cols = query_weight.shape[1]
    positions, kv_both = key_value_cache.shape[1:]
    store, _, rank = adapter_down_pages.shape
    out_cols = adapter_up_pages.shape[2]
    rows = steps * reqs
    chunk_rows = head_cols // HEAD_SIZE // CHUNKS * rows
    dims = (n, steps, reqs, width, head_cols, positions, store, rank, out_cols, CHUNKS, PIECES)
    bf16, f32 = jnp.bfloat16, jnp.float32
    dma = pltpu.SemaphoreType.DMA
    vmem = pl.BlockSpec(memory_space=pltpu.VMEM)
    smem = pl.BlockSpec(memory_space=pltpu.SMEM)
    hbm = pl.BlockSpec(memory_space=pl.ANY)
    return pl.pallas_call(
        functools.partial(fused_kernel, dims),
        out_shape=jax.ShapeDtypeStruct((steps, reqs, out_cols), bf16),
        in_specs=[vmem, vmem, hbm, hbm, hbm, hbm, hbm, smem, smem, smem, smem, hbm, hbm],
        out_specs=vmem,
        scratch_shapes=[
            pltpu.VMEM((width, head_cols), bf16),
            pltpu.VMEM((width, HEAD_SIZE), bf16),
            pltpu.VMEM((width, HEAD_SIZE), bf16),
            pltpu.VMEM((n, head_cols, out_cols), bf16),
            pltpu.VMEM((reqs, positions, kv_both), bf16),
            pltpu.VMEM((2, positions, kv_both), bf16),
            pltpu.VMEM((2, positions, kv_both), bf16),
            pltpu.VMEM((n, reqs * positions, HEAD_SIZE), bf16),
            pltpu.VMEM((n, reqs * positions, HEAD_SIZE), bf16),
            pltpu.VMEM((store, rank, head_cols), bf16),
            pltpu.VMEM((store, rank, out_cols), bf16),
            pltpu.VMEM((reqs, rank, head_cols), bf16),
            pltpu.VMEM((reqs, rank, out_cols), bf16),
            pltpu.VMEM((reqs, rank, head_cols), bf16),
            pltpu.VMEM((reqs, rank, out_cols), bf16),
            pltpu.VMEM((rows, width), f32),
            pltpu.VMEM((rows, width), bf16),
            pltpu.VMEM((CHUNKS, n, chunk_rows, HEAD_SIZE), bf16),
            pltpu.VMEM((CHUNKS, n, chunk_rows + 16, HEAD_SIZE), bf16),
            pltpu.VMEM((CHUNKS, n, chunk_rows + 16, HEAD_SIZE), bf16),
            pltpu.VMEM((rows, rank), f32),
            pltpu.VMEM((n, rows, rank), f32),
            pltpu.VMEM((n, rows, out_cols), bf16),
            pltpu.VMEM((n, rows, out_cols), bf16),
            dma((CHUNKS, PIECES)),
            dma((2,)),
            dma((n,)),
            dma((3,)),
            dma((3,)),
            dma((3,)),
            dma((CHUNKS, n)),
            dma((CHUNKS, n)),
            dma((CHUNKS, n)),
            dma((CHUNKS, n)),
            dma((n,)),
            dma((n,)),
            dma((n,)),
            dma((n,)),
        ],
        compiler_params=pltpu.CompilerParams(
            collective_id=0, has_side_effects=True, vmem_limit_bytes=60 * 1024 * 1024
        ),
        name="fused",
    )(
        hidden_input,
        input_norm_gain.reshape(width // 128, 128),
        query_weight,
        key_weight,
        value_weight,
        output_weight,
        key_value_cache,
        lengths,
        leaving,
        request_adapter_index,
        adapter_page_table,
        jnp.swapaxes(adapter_down_pages, 1, 2),
        adapter_up_pages,
    )


def solution(mesh):
    body = fused if mesh.shape["tp"] == KVH and mesh.shape["inst"] == 2 else shards
    return jax.shard_map(
        body,
        mesh=mesh,
        in_specs=(
            P(None, ("groups", "inst"), None),
            P(),
            P(None, "tp"),
            P(None, "tp"),
            P(None, "tp"),
            P("tp", None),
            P(("groups", "inst"), "tp", None),
            P("groups"),
            P("groups", None),
            P("groups"),
            P(),
            P("inst", "tp", None),
            P("inst", None, "tp"),
        ),
        out_specs=P(None, ("groups", "inst"), "tp"),
        check_vma=False,
    )
```
